32 devices in a mesh: gx: 4 (over y, x), gy: 2 (over core), gz: 4 (over z).
Axes of the slice: x: 2, y: 2, z: 4, core: 2. Of those that a mesh axis runs over, the one named last changes fastest.
Arguments:
- density: float32 [96, 128, 512], P('gx', 'gy', 'gz'), may hold values from 0.8 to 1.25
- momentum: float32 [3, 96, 128, 512], P(None, 'gx', 'gy', 'gz'), may hold values from -1.5 to 1.5
- energy: float32 [96, 128, 512], P('gx', 'gy', 'gz'), may hold values from 2 to 3
- increment: float32 [5, 96, 128, 512], P(None, 'gx', 'gy', 'gz'), may hold values from -1.8 to 1.8
Outputs:
- new_state: float32 [5, 96, 128, 512], P(None, 'gx', 'gy', 'gz')
- new_increment: float32 [5, 96, 128, 512], P(None, 'gx', 'gy', 'gz')
The draws below stay inside these ranges and needn't reach their ends.
All inputs are finite; a program needn't handle non-finite values.
Results may differ from the reference program's by a relative error of at most 0.0003.
Values sent between devices are 32-bit elements; how exact they have to be, the bound alone decides.
No kernel may reach another device: no remote copies, remote signals or barrier semaphores. Data moves between devices by JAX's collectives and lax.ppermute only.
A program may use at most 128 MiB of HBM per device.

```python
import math
import jax
import jax.numpy as jnp
from jax import lax

NVAR = 5
NX = 96
NY = 128
NZ = 512


def banded_field(key, lower, upper):
    return jax.random.uniform(key, (NX, NY, NZ), jnp.float32, lower, upper)


def draw_density(key, part):
    return banded_field(jax.random.fold_in(key, 11), 0.8, 1.25)


def draw_energy(key, part):
    return banded_field(jax.random.fold_in(key, 23), 2.0, 3.0)


def block_scale(rng, dims, cuts, low, top_value):
    def one(position, shards_of):
        draws = jax.random.uniform(jax.random.fold_in(jax.random.fold_in(rng, 6), position), (shards_of,), jnp.float32, low / len(cuts), top_value / len(cuts))
        return jnp.repeat(jnp.exp(draws), dims[position] // shards_of).reshape((-1,) + (1,) * (len(dims) - position - 1))

    level = one(*cuts[0])
    for cut in cuts[1:]:
        level = level * one(*cut)
    return level


def gaussian(key, shape, width, most, shards=(), kind=jnp.bfloat16):
    gain = block_scale(key, shape, shards, -0.22, 0.18) if shards else 1.0
    result = jax.random.normal(key, shape, jnp.float32) * width * gain
    return jnp.minimum(jnp.maximum(result, -most), most).astype(kind)


def setup_inputs(seed: int = 0) -> dict:
    keys = jax.random.split(jax.random.key(seed), 5)
    return {
        "density": draw_density(jax.random.fold_in(keys[4], 71), 0),
        "momentum": gaussian(keys[1], (3, NX, NY, NZ), 0.3, 1.5, ((1, 4), (2, 2), (3, 4)), jnp.float32),
        "energy": draw_energy(jax.random.fold_in(keys[4], 71), 0),
        "increment": gaussian(keys[3], (NVAR, NX, NY, NZ), 0.3, 1.8, ((1, 4), (2, 2), (3, 4)), jnp.float32),
    }


deriv_alpha = 1.0 / 3.0
filter_alpha = 0.4999
gas_gamma = 1.4
time_step = 0.2
section_a = -5.0 / 9.0
section_b = 15.0 / 16.0

def root_of(coupling):
    return (-1.0 + math.sqrt(1.0 - 4.0 * coupling * coupling)) / (2.0 * coupling)

def signed_power(base_value, exponent):
    magnitude = jnp.power(jnp.float32(abs(base_value)), exponent.astype(jnp.float32))
    if base_value < 0:
        return jnp.where(exponent % 2 == 0, 1.0, -1.0).astype(jnp.float32) * magnitude
    return magnitude

def filter_weights(coupling):
    return [(93.0 + 70.0 * coupling) / 128.0, (7.0 + 18.0 * coupling) / 16.0, (-7.0 + 14.0 * coupling) / 32.0, (1.0 - 2.0 * coupling) / 16.0, (-1.0 + 2.0 * coupling) / 128.0]

def fluxes(cell_block, axis_k):
    density = cell_block[0]
    momentum = cell_block[1:4]
    energy = cell_block[4]
    squared = momentum[0] * momentum[0] + momentum[1] * momentum[1] + momentum[2] * momentum[2]
    pressure = (gas_gamma - 1.0) * (energy - 0.5 * squared / density)
    velocity = momentum[axis_k] / density
    components = [momentum[axis_k], momentum[0] * velocity, momentum[1] * velocity, momentum[2] * velocity, (energy + pressure) * velocity]
    components[axis_k + 1] = components[axis_k + 1] + pressure
    return jnp.stack(components)

def periodic_solve(right_side, coupling):
    decay_rate = root_of(coupling)
    length = right_side.shape[1]
    lines_first = jnp.moveaxis(right_side, 1, 0)

    def advance(previous, element):
        updated = element + decay_rate * previous
        return (updated, updated)
    zero_start = jnp.zeros(lines_first.shape[1:], jnp.float32)
    last_value, forward = lax.scan(advance, zero_start, lines_first)
    closure = 1.0 - decay_rate ** length
    positions = jnp.arange(length, dtype=jnp.int32)
    broadcast_shape = (length,) + (1,) * (lines_first.ndim - 1)
    forward = forward + signed_power(decay_rate, positions + 1).reshape(broadcast_shape) * (last_value / closure)[None]
    first_value, backward = lax.scan(advance, zero_start, forward, reverse=True)
    backward = backward + signed_power(decay_rate, length - positions).reshape(broadcast_shape) * (first_value / closure)[None]
    return jnp.moveaxis(-(decay_rate / coupling) * backward, 0, 1)

def explicit_derivative(field, along_axis):
    summed = jnp.zeros_like(field)
    for offset, weight_n in ((1, 0.75), (2, -0.15), (3, 1.0 / 60.0)):
        summed = summed + weight_n * (jnp.roll(field, -offset, along_axis) - jnp.roll(field, offset, along_axis))
    return summed

def reference(density, momentum, energy, increment):
    fluid_state = jnp.concatenate([density[None], momentum, energy[None]], axis=0)
    flux_x = fluxes(fluid_state, 0)
    compact_side = 7.0 / 9.0 * (jnp.roll(flux_x, -1, 1) - jnp.roll(flux_x, 1, 1)) + 1.0 / 36.0 * (jnp.roll(flux_x, -2, 1) - jnp.roll(flux_x, 2, 1))
    spatial = periodic_solve(compact_side, deriv_alpha)
    spatial = spatial + explicit_derivative(fluxes(fluid_state, 1), 2)
    spatial = spatial + explicit_derivative(fluxes(fluid_state, 2), 3)
    new_increment = section_a * increment - time_step * spatial
    provisional = fluid_state + section_b * new_increment
    weights = filter_weights(filter_alpha)
    filter_side = weights[0] * provisional
    for offset in range(1, 5):
        filter_side = filter_side + weights[offset] / 2.0 * (jnp.roll(provisional, -offset, 1) + jnp.roll(provisional, offset, 1))
    new_state = periodic_solve(filter_side, filter_alpha)
    return (new_state, new_increment)
```

```python
import functools
import math

import jax
import jax.numpy as jnp
import numpy as np
from jax import lax
from jax.experimental import pallas as pl
from jax.experimental.pallas import tpu as pltpu
from jax.sharding import PartitionSpec as P

deriv_alpha = 1.0 / 3.0
filter_alpha = 0.4999
gas_gamma = 1.4
time_step = 0.2
section_a = -5.0 / 9.0
section_b = 15.0 / 16.0
explicit_weights = (0.75, -0.15, 1.0 / 60.0)
f32 = jnp.float32


def root_of(coupling):
    return (-1.0 + math.sqrt(1.0 - 4.0 * coupling * coupling)) / (2.0 * coupling)


def laurent(poly, times_s):
    size = len(poly) + 1
    total = np.zeros(2 * size + 1)
    for power, value in enumerate(poly):
        term = np.array([1.0])
        for _ in range(power):
            term = np.convolve(term, [1.0, 0.0, 1.0])
        if times_s:
            term = np.convolve(term, [-1.0, 0.0, 1.0])
        half = len(term) // 2
        total[size - half : size + half + 1] += value * term
    return [float(v) for v in total[size:]]


def x_constants():
    ad, af = deriv_alpha, filter_alpha
    kappa = (1.0 / 36.0) / ad
    beta = 7.0 / 9.0 - kappa
    poly = np.polynomial.polynomial
    p_of_c = (1.0 - 2.0 * af) / 256.0 * poly.polypow([2.0, -1.0], 4)
    q_of_c, rest = poly.polydiv(p_of_c, [1.0, af])
    rho = float(rest[0])
    both = poly.polymul([1.0, af], [1.0, ad])
    q2_of_c, _ = poly.polydiv(p_of_c, both)
    mu_f = float(poly.polyval(-1.0 / af, p_of_c)) / (1.0 - ad / af)
    mu_d = float(poly.polyval(-1.0 / ad, p_of_c)) / (1.0 - af / ad)
    b_of_c = poly.polyadd(kappa * q_of_c, beta * q2_of_c)
    g = 1.0 / math.sqrt(1.0 - 4.0 * af * af)
    sigma = -section_b * time_step
    return dict(
        kappa=kappa,
        deriv=beta / ad,
        band_q=laurent(q_of_c, False)[:4],
        band_f=[sigma * v for v in laurent(b_of_c, True)[:5]],
        own=rho * g,
        pair=sigma * (kappa * rho + beta * mu_f) / af,
        slow=sigma * beta * mu_d / ad,
    )


X = x_constants()
ROOT_D = root_of(deriv_alpha)
ROOT_F = root_of(filter_alpha)


def primitives(cells):
    density, m0, m1, m2, energy = cells
    inverse = 1.0 / density
    squared = m0 * m0 + m1 * m1 + m2 * m2
    pressure = (gas_gamma - 1.0) * (energy - 0.5 * squared * inverse)
    return inverse, pressure


def flux(cells, inverse, pressure, axis_k):
    momentum = cells[1:4]
    velocity = momentum[axis_k] * inverse
    parts = [
        momentum[axis_k],
        momentum[0] * velocity,
        momentum[1] * velocity,
        momentum[2] * velocity,
        (cells[4] + pressure) * velocity,
    ]
    parts[axis_k + 1] = parts[axis_k + 1] + pressure
    return parts


def lanes(shape):
    return lax.broadcasted_iota(jnp.int32, shape, len(shape) - 1)


def roll(value, amount):
    size = value.shape[-1]
    if isinstance(amount, int):
        amount = amount % size
        if amount == 0:
            return value
    return pltpu.roll(value, amount, value.ndim - 1)


def edge_kernel(rho, mom, ene, up, down, z_up, z_down, z_own, y_edge):
    nx, rows, nz = rho.shape
    lane = lanes((8, nz))
    slot = lane // 8
    first_half = lane % 8 < 4

    def tile(t, _):
        at = pl.ds(pl.multiple_of(8 * t, 8), 8)
        lower = upper = None
        packed = [[None] * 5, [None] * 5]
        for x in range(nx):
            cells = [rho[x, at], mom[0, x, at], mom[1, x, at], mom[2, x, at], ene[x, at]]
            inverse, pressure = primitives(cells)
            f = flux(cells, inverse, pressure, 0)
            if x == 0:
                lower, upper = f, f
                for v in range(5):
                    down[0, v, at] = f[v]
            else:
                lower = [ROOT_D * a + b for a, b in zip(lower, f)]
                upper = [a + ROOT_D**x * b for a, b in zip(upper, f)]
            if x == nx - 1:
                for v in range(5):
                    up[0, v, at] = f[v]
            group, place = x // 16, x % 16
            for v in range(5):
                moved = roll(cells[v], 8 * place + 3)
                if place:
                    moved = jnp.where(slot == place, moved, packed[group][v])
                packed[group][v] = moved
        for v in range(5):
            up[1, v, at] = lower[v]
            down[1, v, at] = upper[v]
        h = []
        for group in range(2):
            inverse, pressure = primitives(packed[group])
            h.append(flux(packed[group], inverse, pressure, 2))
            for v in range(5):
                z_own[group, v, at] = h[group][v]
        for v in range(5):
            z_up[v, at] = jnp.where(first_half, h[0][v], roll(h[1][v], 4))
            z_down[v, at] = jnp.where(first_half, roll(h[0][v], -3), roll(h[1][v], 1))
        return 0

    lax.fori_loop(0, rows // 8, tile, 0)

    def edge_rows(at):
        for x in range(nx):
            cells = [rho[x, at], mom[0, x, at], mom[1, x, at], mom[2, x, at], ene[x, at]]
            inverse, pressure = primitives(cells)
            yield x, flux(cells, inverse, pressure, 1)

    @pl.when(pl.program_id(0) == 0)
    def _():
        for x, g in edge_rows(slice(0, 8)):
            for v in range(5):
                y_edge[v, x] = g[v]

    @pl.when(pl.program_id(0) == pl.num_programs(0) - 1)
    def _():
        first = lax.broadcasted_iota(jnp.int32, (8, nz), 0) < 4
        for x, g in edge_rows(slice(rows - 8, rows)):
            for v in range(5):
                y_edge[v, x] = jnp.where(first, y_edge[v, x], g[v])


def cross_kernel(
    rho, mom, ene, inc, y_halo, z_low, z_high, z_own,
    part, sums, w_up, w_down, fix, pad, f_row, power,
):
    nx, ny, nz = rho.shape
    step = pl.program_id(0)
    lane = lanes((8, nz))
    edge_lane = (lane < 3) | (lane >= nz - 3)
    w1, w2, w3 = explicit_weights

    @pl.when(step == 0)
    def _():
        place = lane % 8
        for t in range(ny // 8):
            at = slice(8 * t, 8 * t + 8)
            for v in range(5):
                low, high = z_low[v, at], z_high[v, at]
                for group in range(2):
                    own = z_own[group, v, at]
                    below = roll(low, -4) if group else low
                    above = roll(high, -1) if group else roll(high, 3)
                    below = jnp.where(place < 3, below - own, 0.0)
                    above = jnp.where((place >= 3) & (place < 6), above - own, 0.0)
                    last = w1 * roll(above, -1) + w2 * roll(above, -2) + w3 * roll(above, -3)
                    first = w1 * roll(below, 1) + w2 * roll(below, 2) + w3 * roll(below, 3)
                    fix[group, v, at] = jnp.where(place < 3, last, -first)
        sums[...] = jnp.zeros_like(sums)
        power[...] = jnp.ones_like(power)

    def one_row(i, _):
        x = step * nx + i
        turn = lax.rem(nz + nz - 3 - 8 * lax.rem(x, 16), nz)
        group = x // 16
        for v in range(5):
            pad[v, 0:8] = y_halo[v, i]
            pad[v, ny + 8 : ny + 16] = y_halo[v, i]
        for t in range(ny // 8):
            at = slice(8 * t, 8 * t + 8)
            cells = [rho[i, at], mom[0, i, at], mom[1, i, at], mom[2, i, at], ene[i, at]]
            inverse, pressure = primitives(cells)
            f = flux(cells, inverse, pressure, 0)
            g = flux(cells, inverse, pressure, 1)
            h = flux(cells, inverse, pressure, 2)
            for v in range(5):
                f_row[v, at] = f[v]
                pad[v, 8 + 8 * t : 16 + 8 * t] = g[v]
                dz = (
                    w1 * (roll(h[v], -1) - roll(h[v], 1))
                    + w2 * (roll(h[v], -2) - roll(h[v], 2))
                    + w3 * (roll(h[v], -3) - roll(h[v], 3))
                )
                dz = dz + jnp.where(edge_lane, roll(fix[group, v, at], turn), 0.0)
                part[v, i, at] = section_a * inc[v, i, at] - time_step * dz
        scale = power[...]
        for t in range(ny // 8):
            at = slice(8 * t, 8 * t + 8)
            state = [rho[i, at], mom[0, i, at], mom[1, i, at], mom[2, i, at], ene[i, at]]
            for v in range(5):

                def g_at(n, v=v, t=t):
                    return pad[v, 8 + 8 * t + n : 16 + 8 * t + n]

                dy = (
                    w1 * (g_at(1) - g_at(-1))
                    + w2 * (g_at(2) - g_at(-2))
                    + w3 * (g_at(3) - g_at(-3))
                )
                value = part[v, i, at] - time_step * dy
                part[v, i, at] = value
                q = X["own"] * (state[v] + section_b * value)
                f = X["pair"] * f_row[v, at]
                sums[0, v, at] = ROOT_F * sums[0, v, at] + (q + f)
                sums[1, v, at] = sums[1, v, at] + scale * (q - f)
        power[...] = scale * ROOT_F
        return 0

    lax.fori_loop(0, nx, one_row, 0)

    def halo(out, near, sign):
        def tile(t, _):
            at = pl.ds(pl.multiple_of(8 * t, 8), 8)
            total = [[None] * 5 for _ in range(3)]
            for j in range(1, 5):
                i = near(j)
                cells = [rho[i, at], mom[0, i, at], mom[1, i, at], mom[2, i, at], ene[i, at]]
                inverse, pressure = primitives(cells)
                f = flux(cells, inverse, pressure, 0)
                for v in range(5):
                    q = cells[v] + section_b * part[v, i, at]
                    for k in range(3):
                        n = k + j
                        if n > 4:
                            continue
                        term = (sign * X["band_f"][n]) * f[v]
                        if n <= 3:
                            term = term + X["band_q"][n] * q
                        total[k][v] = term if total[k][v] is None else total[k][v] + term
            for k in range(3):
                for v in range(5):
                    out[k, v, at] = total[k][v]
            return 0

        lax.fori_loop(0, ny // 8, tile, 0)

    @pl.when(step == 0)
    def _():
        halo(w_down, lambda j: j - 1, 1.0)

    @pl.when(step == pl.num_programs(0) - 1)
    def _():
        halo(w_up, lambda j: nx - j, -1.0)


def line_kernel(rho, mom, ene, part, from_low, from_high, far, new_inc, local, f_all, q_all, e_all):
    nx = rho.shape[0]

    def fluxes_at(x, _):
        cells = [rho[x], mom[0, x], mom[1, x], mom[2, x], ene[x]]
        inverse, pressure = primitives(cells)
        for v, value in enumerate(flux(cells, inverse, pressure, 0)):
            f_all[v, x] = value
            q_all[v, x] = cells[v] + section_b * part[v, x]
        return 0

    lax.fori_loop(0, nx, fluxes_at, 0)

    def one(v, _):
        f = [f_all[v, x] for x in range(nx)]
        q = [q_all[v, x] for x in range(nx)]
        low, high = from_low[0, v], from_high[0, v]
        forward = ROOT_D * far[0, v]
        for x in range(nx):
            e_all[x] = forward
            forward = ROOT_D * (f[x] + forward)
        backward = ROOT_D * far[1, v]
        for x in reversed(range(nx)):
            e_all[x] = e_all[x] - backward
            backward = ROOT_D * (f[x] + backward)
        ahead = None
        for x in range(nx):
            before = low if x == 0 else f[x - 1]
            after = high if x == nx - 1 else f[x + 1]
            e = e_all[x]
            deriv = X["kappa"] * (after - before) + X["deriv"] * e
            new_inc[v, x] = part[v, x] - time_step * deriv
            total = (1.0 - X["band_q"][0] - X["own"]) * q[x] - X["slow"] * e
            total = total - (section_b * time_step) * deriv
            for n in range(1, 4):
                near = [q[i] for i in (x - n, x + n) if 0 <= i < nx]
                total = total - X["band_q"][n] * (near[0] if len(near) == 1 else near[0] + near[1])
            for n in range(1, 5):
                if x + n < nx and x - n >= 0:
                    total = total - X["band_f"][n] * (f[x + n] - f[x - n])
                elif x + n < nx:
                    total = total - X["band_f"][n] * f[x + n]
                else:
                    total = total + X["band_f"][n] * f[x - n]
            if x == 3:
                total = total + X["band_f"][4] * low
            if x == nx - 4:
                total = total - X["band_f"][4] * high
            if ahead is not None:
                total = total - ahead
            local[v, x] = total
            plus = X["own"] * q[x] + X["pair"] * f[x]
            ahead = ROOT_F * (plus if ahead is None else plus + ahead)
        behind = None
        for x in reversed(range(nx)):
            if behind is not None:
                local[v, x] = local[v, x] - behind
            minus = X["own"] * q[x] - X["pair"] * f[x]
            behind = ROOT_F * (minus if behind is None else minus + behind)
        return 0

    lax.fori_loop(0, 5, one, 0)


def final_kernel(local, incoming, w_low, w_high, out):
    nx = local.shape[1]

    def one(v, _):
        low, high = incoming[0, v], incoming[1, v]
        for x in range(nx):
            value = local[v, x] - (ROOT_F ** (x + 1)) * low - (ROOT_F ** (nx - x)) * high
            if x < 3:
                value = value - w_low[x, v]
            if x >= nx - 3:
                value = value - w_high[nx - 1 - x, v]
            out[v, x] = value
        return 0

    lax.fori_loop(0, 5, one, 0)


def shifted(value, axis, by):
    size = lax.axis_size(axis)
    return lax.ppermute(value, axis, [(i, (i + by) % size) for i in range(size)])


def ring_sums(own, rate):
    size = lax.axis_size("gx")
    gathered = lax.all_gather(own, "gx", axis=0)
    here = lax.axis_index("gx")
    member = jnp.arange(size, dtype=jnp.int32)
    table = jnp.asarray([rate**k / (1.0 - rate**size) for k in range(size)], f32)
    up = table[(here - 1 - member) % size]
    down = table[(member - here - 1) % size]
    shape = (size,) + (1,) * (own.ndim - 1)
    low = jnp.sum(up.reshape(shape) * gathered[:, 0], axis=0)
    high = jnp.sum(down.reshape(shape) * gathered[:, 1], axis=0)
    return jnp.stack([low, high])


def block(shape, index):
    return pl.BlockSpec(shape, index)


def on_device(density, momentum, energy, increment):
    nx, ny, nz = density.shape
    members = lax.axis_size("gx")
    cells = nx * ny * nz
    params = pltpu.CompilerParams(vmem_limit_bytes=40 * 2**20)

    def shape(*dims):
        return jax.ShapeDtypeStruct(dims, f32)

    rows = 16
    state_by_y = [
        block((nx, rows, nz), lambda i: (0, i, 0)),
        block((3, nx, rows, nz), lambda i: (0, 0, i, 0)),
        block((nx, rows, nz), lambda i: (0, i, 0)),
    ]
    up, down, z_up, z_down, z_own, y_edge = pl.pallas_call(
        edge_kernel,
        grid=(ny // rows,),
        in_specs=state_by_y,
        out_specs=[
            block((2, 5, rows, nz), lambda i: (0, 0, i, 0)),
            block((2, 5, rows, nz), lambda i: (0, 0, i, 0)),
            block((5, rows, nz), lambda i: (0, i, 0)),
            block((5, rows, nz), lambda i: (0, i, 0)),
            block((2, 5, rows, nz), lambda i: (0, 0, i, 0)),
            block((5, nx, 8, nz), lambda i: (0, 0, 0, 0)),
        ],
        out_shape=[
            shape(2, 5, ny, nz),
            shape(2, 5, ny, nz),
            shape(5, ny, nz),
            shape(5, ny, nz),
            shape(2, 5, ny, nz),
            shape(5, nx, 8, nz),
        ],
        compiler_params=params,
        cost_estimate=pl.CostEstimate(flops=60 * cells, bytes_accessed=24 * cells, transcendentals=0),
        name="edges",
    )(density, momentum, energy)

    z_low = shifted(z_up, "gz", 1)
    z_high = shifted(z_down, "gz", -1)
    y_halo = shifted(y_edge, "gy", 1)
    from_low = shifted(up, "gx", 1)
    from_high = shifted(down, "gx", -1)

    some = 4
    keep = lambda *dims: block(dims, lambda i: (0,) * len(dims))
    part, sums, w_up, w_down = pl.pallas_call(
        cross_kernel,
        grid=(nx // some,),
        in_specs=[
            block((some, ny, nz), lambda i: (i, 0, 0)),
            block((3, some, ny, nz), lambda i: (0, i, 0, 0)),
            block((some, ny, nz), lambda i: (i, 0, 0)),
            block((5, some, ny, nz), lambda i: (0, i, 0, 0)),
            block((5, some, 8, nz), lambda i: (0, i, 0, 0)),
            keep(5, ny, nz),
            keep(5, ny, nz),
            keep(2, 5, ny, nz),
        ],
        out_specs=[
            block((5, some, ny, nz), lambda i: (0, i, 0, 0)),
            keep(2, 5, ny, nz),
            keep(3, 5, ny, nz),
            keep(3, 5, ny, nz),
        ],
        out_shape=[
            shape(5, nx, ny, nz),
            shape(2, 5, ny, nz),
            shape(3, 5, ny, nz),
            shape(3, 5, ny, nz),
        ],
        scratch_shapes=[
            pltpu.VMEM((2, 5, ny, nz), f32),
            pltpu.VMEM((5, ny + 16, nz), f32),
            pltpu.VMEM((5, ny, nz), f32),
            pltpu.VMEM((8, nz), f32),
        ],
        compiler_params=params,
        cost_estimate=pl.CostEstimate(flops=240 * cells, bytes_accessed=64 * cells, transcendentals=0),
        name="cross",
    )(density, momentum, energy, increment, y_halo, z_low, z_high, z_own)

    rate_d, rate_f = ROOT_D**nx, ROOT_F**nx
    w_low = shifted(w_up, "gx", 1)
    w_high = shifted(w_down, "gx", -1)
    if members == 4:
        own = jnp.stack([up[1], down[1]])
        beside = jnp.stack([from_low[1], from_high[1]])
        across = shifted(own + rate_d * beside, "gx", 2)
        far = (beside + rate_d * across + rate_d**3 * own) * (1.0 / (1.0 - rate_d**4))
        opposite = shifted(sums, "gx", 2)
        mixed = sums + rate_f**2 * opposite
        beside = jnp.stack([shifted(mixed[0], "gx", 1), shifted(mixed[1], "gx", -1)])
        incoming = (beside + rate_f * opposite + rate_f**3 * sums) * (1.0 / (1.0 - rate_f**4))
    else:
        far = ring_sums(jnp.stack([up[1], down[1]]), rate_d)
        incoming = ring_sums(sums, rate_f)

    lines = 8
    state_by_y = [
        block((nx, lines, nz), lambda i: (0, i, 0)),
        block((3, nx, lines, nz), lambda i: (0, 0, i, 0)),
        block((nx, lines, nz), lambda i: (0, i, 0)),
    ]
    all_lines = block((5, nx, lines, nz), lambda i: (0, 0, i, 0))
    pair = block((2, 5, lines, nz), lambda i: (0, 0, i, 0))
    new_increment, local = pl.pallas_call(
        line_kernel,
        grid=(ny // lines,),
        in_specs=state_by_y + [all_lines, pair, pair, pair],
        out_specs=[all_lines, all_lines],
        out_shape=[shape(5, nx, ny, nz), shape(5, nx, ny, nz)],
        scratch_shapes=[
            pltpu.VMEM((5, nx, lines, nz), f32),
            pltpu.VMEM((5, nx, lines, nz), f32),
            pltpu.VMEM((nx, lines, nz), f32),
        ],
        compiler_params=params,
        cost_estimate=pl.CostEstimate(flops=280 * cells, bytes_accessed=80 * cells, transcendentals=0),
        name="lines",
    )(density, momentum, energy, part, from_low, from_high, far)

    rows = 16
    all_rows = block((5, nx, rows, nz), lambda i: (0, 0, i, 0))
    three = block((3, 5, rows, nz), lambda i: (0, 0, i, 0))
    new_state = pl.pallas_call(
        final_kernel,
        grid=(ny // rows,),
        in_specs=[all_rows, block((2, 5, rows, nz), lambda i: (0, 0, i, 0)), three, three],
        out_specs=all_rows,
        out_shape=shape(5, nx, ny, nz),
        compiler_params=params,
        cost_estimate=pl.CostEstimate(flops=20 * cells, bytes_accessed=44 * cells, transcendentals=0),
        name="final",
    )(local, incoming, w_low, w_high)
    return (new_state, new_increment)


def solution(mesh):
    in_specs = (
        P("gx", "gy", "gz"),
        P(None, "gx", "gy", "gz"),
        P("gx", "gy", "gz"),
        P(None, "gx", "gy", "gz"),
    )
    out_specs = (P(None, "gx", "gy", "gz"), P(None, "gx", "gy", "gz"))
    return jax.shard_map(
        on_device, mesh=mesh, in_specs=in_specs, out_specs=out_specs, check_vma=False
    )
```

```python
import functools
import math

import jax
import jax.numpy as jnp
import numpy as np
from jax import lax
from jax.experimental import pallas as pl
from jax.experimental.pallas import tpu as pltpu
from jax.sharding import PartitionSpec as P

deriv_alpha = 1.0 / 3.0
filter_alpha = 0.4999
gas_gamma = 1.4
time_step = 0.2
section_a = -5.0 / 9.0
section_b = 15.0 / 16.0
explicit_weights = (0.75, -0.15, 1.0 / 60.0)
f32 = jnp.float32


def root_of(coupling):
    return (-1.0 + math.sqrt(1.0 - 4.0 * coupling * coupling)) / (2.0 * coupling)


def laurent(poly, times_s):
    size = len(poly) + 1
    total = np.zeros(2 * size + 1)
    for power, value in enumerate(poly):
        term = np.array([1.0])
        for _ in range(power):
            term = np.convolve(term, [1.0, 0.0, 1.0])
        if times_s:
            term = np.convolve(term, [-1.0, 0.0, 1.0])
        half = len(term) // 2
        total[size - half : size + half + 1] += value * term
    return [float(v) for v in total[size:]]


def x_constants():
    ad, af = deriv_alpha, filter_alpha
    kappa = (1.0 / 36.0) / ad
    beta = 7.0 / 9.0 - kappa
    poly = np.polynomial.polynomial
    p_of_c = (1.0 - 2.0 * af) / 256.0 * poly.polypow([2.0, -1.0], 4)
    q_of_c, rest = poly.polydiv(p_of_c, [1.0, af])
    rho = float(rest[0])
    both = poly.polymul([1.0, af], [1.0, ad])
    q2_of_c, _ = poly.polydiv(p_of_c, both)
    mu_f = float(poly.polyval(-1.0 / af, p_of_c)) / (1.0 - ad / af)
    mu_d = float(poly.polyval(-1.0 / ad, p_of_c)) / (1.0 - af / ad)
    b_of_c = poly.polyadd(kappa * q_of_c, beta * q2_of_c)
    g = 1.0 / math.sqrt(1.0 - 4.0 * af * af)
    sigma = -section_b * time_step
    return dict(
        kappa=kappa,
        deriv=beta / ad,
        band_q=laurent(q_of_c, False)[:4],
        band_f=[sigma * v for v in laurent(b_of_c, True)[:5]],
        own=rho * g,
        pair=sigma * (kappa * rho + beta * mu_f) / af,
        slow=sigma * beta * mu_d / ad,
    )


X = x_constants()
ROOT_D = root_of(deriv_alpha)
ROOT_F = root_of(filter_alpha)


def primitives(cells):
    density, m0, m1, m2, energy = cells
    inverse = 1.0 / density
    squared = m0 * m0 + m1 * m1 + m2 * m2
    pressure = (gas_gamma - 1.0) * (energy - 0.5 * squared * inverse)
    return inverse, pressure


def flux(cells, inverse, pressure, axis_k):
    momentum = cells[1:4]
    velocity = momentum[axis_k] * inverse
    parts = [
        momentum[axis_k],
        momentum[0] * velocity,
        momentum[1] * velocity,
        momentum[2] * velocity,
        (cells[4] + pressure) * velocity,
    ]
    parts[axis_k + 1] = parts[axis_k + 1] + pressure
    return parts


def lanes(shape):
    return lax.broadcasted_iota(jnp.int32, shape, len(shape) - 1)


def roll(value, amount):
    size = value.shape[-1]
    if isinstance(amount, int):
        amount = amount % size
        if amount == 0:
            return value
    return pltpu.roll(value, amount, value.ndim - 1)


def cells_at(rho, mom, ene, x, at):
    return [rho[x, at], mom[0, x, at], mom[1, x, at], mom[2, x, at], ene[x, at]]


class Blocks:
    def __init__(self, sources, targets, sems, dims, size, begin=0):
        self.copies = []
        for k in range(targets[0].shape[dims[0]] // size):
            piece = []
            for n, (source, target, dim) in enumerate(zip(sources, targets, dims)):
                lead = (slice(None),) * dim
                there = source.at[(*lead, pl.ds(begin + k * size, size))]
                here = target.at[(*lead, pl.ds(k * size, size))]
                piece.append(pltpu.make_async_copy(there, here, sems.at[n, k]))
            self.copies.append(piece)
        for piece in self.copies:
            for copy in piece:
                copy.start()

    def wait(self, k):
        for copy in self.copies[k]:
            copy.wait()


def cells_at(rho, mom, ene, x, at):
    return [rho[x, at], mom[0, x, at], mom[1, x, at], mom[2, x, at], ene[x, at]]


def face_kernel(
    rho_hbm, mom_hbm, ene_hbm,
    up, down, own, g_rows, h_rows, z_up, z_down, z_own, y_edge, token,
    rho, mom, ene, sems,
):
    nx, ny, nz = rho.shape
    lane = lanes((8, nz))
    slot = lane // 8
    first_half = lane % 8 < 4
    row = lax.broadcasted_iota(jnp.int32, (8, nz), 0)
    stored = {x: r for r, x in enumerate((0, 1, 2, nx - 3, nx - 2, nx - 1))}
    rows = 16
    blocks = Blocks((rho_hbm, mom_hbm, ene_hbm), (rho, mom, ene), sems, (1, 2, 1), rows)
    token[...] = jnp.zeros_like(token)

    def tile(t, _):
        at = pl.ds(pl.multiple_of(8 * t, 8), 8)
        keep = (row < 4) & (t > 0)
        packed = [[None] * 5, [None] * 5]
        totals = lower = upper = None
        for x in range(nx):
            cells = cells_at(rho, mom, ene, x, at)
            inverse, pressure = primitives(cells)
            f = flux(cells, inverse, pressure, 0)
            g = flux(cells, inverse, pressure, 1)
            h = flux(cells, inverse, pressure, 2)
            group, place = x // 16, x % 16
            for v in range(5):
                y_edge[v, x] = jnp.where(keep, y_edge[v, x], g[v])
                moved = roll(cells[v], 8 * place + 3)
                if place:
                    moved = jnp.where(slot == place, moved, packed[group][v])
                packed[group][v] = moved
                if x in stored:
                    g_rows[stored[x], v, at] = g[v]
                    h_rows[stored[x], v, at] = h[v]
                if x == 0:
                    down[0, v, at] = f[v]
                if x == nx - 1:
                    up[0, v, at] = f[v]
            if x == 0:
                totals, lower, upper = [g, h, g, h], f, f
            else:
                lower = [ROOT_D * a + b for a, b in zip(lower, f)]
                upper = [a + ROOT_D**x * b for a, b in zip(upper, f)]
                factor = ROOT_F**x
                totals = [
                    [ROOT_F * a + b if k < 2 else a + factor * b for a, b in zip(total, term)]
                    for k, (total, term) in enumerate(zip(totals, (g, h, g, h)))
                ]
        h = [flux(packed[group], *primitives(packed[group]), 2) for group in range(2)]
        for v in range(5):
            up[1, v, at] = own[0, v, at] = lower[v]
            down[1, v, at] = own[1, v, at] = upper[v]
            for k in range(2):
                g_rows[6 + k, v, at] = totals[2 * k][v]
                h_rows[6 + k, v, at] = totals[2 * k + 1][v]
                y_edge[v, nx + k] = jnp.where(keep, y_edge[v, nx + k], totals[2 * k][v])
                group, place = (nx + k) // 16, (nx + k) % 16
                moved = roll(totals[2 * k + 1][v], 8 * place + 3)
                h[group][v] = jnp.where(slot == place, moved, h[group][v])
            for group in range(2):
                z_own[group, v, at] = h[group][v]
            z_up[v, at] = jnp.where(first_half, h[0][v], roll(h[1][v], 4))
            z_down[v, at] = jnp.where(first_half, roll(h[0][v], -3), roll(h[1][v], 1))
        return 0

    for k in range(ny // rows):
        blocks.wait(k)
        lax.fori_loop(k * rows // 8, (k + 1) * rows // 8, tile, 0)


def base_kernel(rho_hbm, mom_hbm, ene_hbm, inc_hbm, after, base, w_up, w_down, rho, mom, ene, inc, sems):
    nx, ny, nz = rho.shape
    rows = 16
    blocks = Blocks((rho_hbm, mom_hbm, ene_hbm, inc_hbm), (rho, mom, ene, inc), sems, (1, 2, 1, 2), rows)

    def tile(t, _):
        at = pl.ds(pl.multiple_of(8 * t, 8), 8)
        totals = None
        ends = {1.0: [[None] * 5 for _ in range(3)], -1.0: [[None] * 5 for _ in range(3)]}
        for x in range(nx):
            cells = cells_at(rho, mom, ene, x, at)
            f = flux(cells, *primitives(cells), 0)
            q = [cells[v] + (section_a * section_b) * inc[v, x, at] for v in range(5)]
            own = [X["own"] * q[v] for v in range(5)]
            pair = [X["pair"] * f[v] for v in range(5)]
            plus = [a + b for a, b in zip(own, pair)]
            minus = [a - b for a, b in zip(own, pair)]
            if x == 0:
                totals = [plus, minus]
            else:
                totals[0] = [ROOT_F * a + b for a, b in zip(totals[0], plus)]
                totals[1] = [a + ROOT_F**x * b for a, b in zip(totals[1], minus)]
            for sign, j in ((1.0, x + 1), (-1.0, nx - x)):
                for k in range(3):
                    n = k + j
                    if n > 4:
                        continue
                    for v in range(5):
                        term = (sign * X["band_f"][n]) * f[v]
                        if n <= 3:
                            term = term + X["band_q"][n] * q[v]
                        so_far = ends[sign][k][v]
                        ends[sign][k][v] = term if so_far is None else so_far + term
            if x == 3:
                for k in range(3):
                    for v in range(5):
                        w_down[k, v, at] = ends[1.0][k][v]
        for v in range(5):
            base[0, v, at] = totals[0][v]
            base[1, v, at] = totals[1][v]
            for k in range(3):
                w_up[k, v, at] = ends[-1.0][k][v]
        return 0

    for k in range(ny // rows):
        blocks.wait(k)
        lax.fori_loop(k * rows // 8, (k + 1) * rows // 8, tile, 0)


def fix_table(nz):
    weight = {1: 45.0, 2: -9.0, 3: 1.0}
    table = np.zeros((4 * nz, 2 * nz))
    for group in range(2):
        for place in range(nz // 8):
            into = group * nz + 8 * place
            came = 8 * place + 4 * group
            kept = (2 + group) * nz + 8 * place
            for j in range(3):
                for n, w in weight.items():
                    if j + n >= 3:
                        table[nz + came + j + n - 3, into + j] += w
                        table[kept + 3 + j + n - 3, into + j] -= w
                    if n > j:
                        table[came + 3 + j - n, into + 3 + j] -= w
                        table[kept + 3 + j - n, into + 3 + j] += w
    return table


def split(value):
    high = value.astype(jnp.bfloat16)
    return high, (value - high.astype(f32)).astype(jnp.bfloat16)


def around(at):
    return 45.0 * (at(1) - at(-1)) - 9.0 * (at(2) - at(-2)) + (at(3) - at(-3))


def turn_of(x, nz):
    if isinstance(x, int):
        return (2 * nz - 3 - 8 * (x % 16)) % nz
    return lax.rem(2 * nz - 3 - 8 * lax.rem(x, 16), nz)


def end_kernel(
    base, w_up0, w_down0, g_rows, h_rows, y_halo, z_low, z_high, z_own, table,
    sums, own_sums, w_up, w_down, fix, pad, dz_all,
):
    ny, nz = base.shape[2:]
    nx = y_halo.shape[1] - 2
    lane = lanes((8, nz))
    edge_lane = (lane < 3) | (lane >= nz - 3)
    parts = [z_low[...], z_high[...], z_own[0], z_own[1]]
    halves = [split(p.reshape(5 * ny, nz)) for p in parts]
    fixed = sum(
        jnp.dot(jnp.concatenate([h[k] for h in halves], axis=1), table[...], preferred_element_type=f32)
        for k in range(2)
    )
    for group in range(2):
        fix[group] = fixed[:, group * nz : group * nz + nz].reshape(5, ny, nz)
    rows = [0, 1, 2, nx - 3, nx - 2, nx - 1, nx, nx + 1]
    for r, x in enumerate(rows):
        for v in range(5):
            pad[r, v, 0:8] = y_halo[v, x]
            pad[r, v, ny + 8 : ny + 16] = y_halo[v, x]

    def first(t, _):
        at = pl.ds(pl.multiple_of(8 * t, 8), 8)
        inside = pl.ds(pl.multiple_of(8 * t + 8, 8), 8)
        for r, x in enumerate(rows):
            for v in range(5):
                h = h_rows[r, v, at]
                pad[r, v, inside] = g_rows[r, v, at]
                moved = roll(fix[x // 16, v, at], turn_of(x, nz))
                dz_all[r, v, at] = around(lambda n: roll(h, -n)) + jnp.where(edge_lane, moved, 0.0)
        return 0

    lax.fori_loop(0, ny // 8, first, 0)
    scale = -time_step * section_b / 60.0

    for t in range(ny // 8):
        at = slice(8 * t, 8 * t + 8)

        def cross(r, v, t=t):
            dy = around(lambda n: pad[r, v, 8 + 8 * t + n : 16 + 8 * t + n])
            return scale * (dy + dz_all[r, v, slice(8 * t, 8 * t + 8)])

        for v in range(5):
            for k in range(2):
                sums[k, v, at] = own_sums[k, v, at] = base[k, v, at] + X["own"] * cross(6 + k, v)
            for out, begin, near in ((w_down, w_down0, (0, 1, 2)), (w_up, w_up0, (5, 4, 3))):
                q = [cross(r, v) for r in near]
                for k in range(3):
                    total = begin[k, v, at]
                    for j in range(1, 4 - k):
                        total = total + X["band_q"][k + j] * q[j - 1]
                    out[k, v, at] = total


def part_kernel(begin, rho_hbm, mom_hbm, ene_hbm, inc_hbm, y_halo, fix, *rest):
    part, token, rho, mom, ene, inc, pad, sems = rest[-8:]
    token[...] = jnp.zeros_like(token)
    nx, ny, nz = rho.shape
    lane = lanes((8, nz))
    edge_lane = (lane < 3) | (lane >= nz - 3)
    scale = -time_step / 60.0
    some = 4
    blocks = Blocks((rho_hbm, mom_hbm, ene_hbm, inc_hbm), (rho, mom, ene, inc), sems, (0, 1, 0, 1), some, begin)

    def one_row(x, _):
        turn = turn_of(begin + x, nz)
        group = (begin + x) // 16
        for v in range(5):
            pad[v, 0:8] = y_halo[v, begin + x]
            pad[v, ny + 8 : ny + 16] = y_halo[v, begin + x]
        for t in range(ny // 8):
            at = slice(8 * t, 8 * t + 8)
            cells = cells_at(rho, mom, ene, x, at)
            inverse, pressure = primitives(cells)
            g = flux(cells, inverse, pressure, 1)
            h = flux(cells, inverse, pressure, 2)
            for v in range(5):
                pad[v, 8 + 8 * t : 16 + 8 * t] = g[v]
                dz = around(lambda n, v=v: roll(h[v], -n))
                dz = dz + jnp.where(edge_lane, roll(fix[group, v, at], turn), 0.0)
                part[v, x, at] = section_a * inc[v, x, at] + scale * dz
        for t in range(ny // 8):
            at = slice(8 * t, 8 * t + 8)
            for v in range(5):
                dy = around(lambda n, v=v, t=t: pad[v, 8 + 8 * t + n : 16 + 8 * t + n])
                part[v, x, at] = part[v, x, at] + scale * dy
        return 0

    for k in range(nx // some):
        blocks.wait(k)
        lax.fori_loop(k * some, (k + 1) * some, one_row, 0)


def line_kernel(
    rho_hbm, mom_hbm, ene_hbm, edges, near, part0, part1,
    new_inc, local,
    rho, mom, ene, f_all, q_all, e_all, sems,
):
    nx, ny, nz = rho.shape
    rows = 16
    blocks = Blocks((rho_hbm, mom_hbm, ene_hbm), (rho, mom, ene), sems, (1, 2, 1), rows)
    for k in range(ny // rows):
        blocks.wait(k)
        at = slice(k * rows, (k + 1) * rows)

        def fluxes_at(x, _, at=at, part=part0, begin=0):
            cells = cells_at(rho, mom, ene, begin + x, at)
            for v, value in enumerate(flux(cells, *primitives(cells), 0)):
                f_all[v, begin + x] = value
                q_all[v, begin + x] = cells[v] + section_b * part[v, x, at]
            return 0

        lax.fori_loop(0, nx // 2, fluxes_at, 0)
        lax.fori_loop(0, nx // 2, functools.partial(fluxes_at, part=part1, begin=nx // 2), 0)
        lax.fori_loop(0, 5, functools.partial(one_line, at, (part0, part1), edges, near, new_inc, local, f_all, q_all, e_all), 0)


def one_line(at, part, edges, near, new_inc, local, f_all, q_all, e_all, v, _):
    nx = f_all.shape[1]
    f = [f_all[v, x] for x in range(nx)]
    q = [q_all[v, x] for x in range(nx)]
    low, high = edges[0, v, at], edges[1, v, at]
    forward = ROOT_D * near[0, v, at]
    for x in range(nx):
        e_all[x] = forward
        forward = ROOT_D * (f[x] + forward)
    backward = ROOT_D * near[1, v, at]
    for x in reversed(range(nx)):
        e_all[x] = e_all[x] - backward
        backward = ROOT_D * (f[x] + backward)
    ahead = None
    for x in range(nx):
        before = low if x == 0 else f[x - 1]
        after = high if x == nx - 1 else f[x + 1]
        e = e_all[x]
        deriv = X["kappa"] * (after - before) + X["deriv"] * e
        new_inc[v, x, at] = part[x // (nx // 2)][v, x % (nx // 2), at] - time_step * deriv
        total = (1.0 - X["band_q"][0] - X["own"]) * q[x] - X["slow"] * e
        total = total - (section_b * time_step) * deriv
        for n in range(1, 4):
            near = [q[i] for i in (x - n, x + n) if 0 <= i < nx]
            total = total - X["band_q"][n] * (near[0] if len(near) == 1 else near[0] + near[1])
        for n in range(1, 5):
            if x + n < nx and x - n >= 0:
                total = total - X["band_f"][n] * (f[x + n] - f[x - n])
            elif x + n < nx:
                total = total - X["band_f"][n] * f[x + n]
            else:
                total = total + X["band_f"][n] * f[x - n]
        if x == 3:
            total = total + X["band_f"][4] * low
        if x == nx - 4:
            total = total - X["band_f"][4] * high
        if ahead is not None:
            total = total - ahead
        local[v, x, at] = total
        plus = X["own"] * q[x] + X["pair"] * f[x]
        ahead = ROOT_F * (plus if ahead is None else plus + ahead)
    behind = None
    for x in reversed(range(nx)):
        if behind is not None:
            local[v, x, at] = local[v, x, at] - behind
        minus = X["own"] * q[x] - X["pair"] * f[x]
        behind = ROOT_F * (minus if behind is None else minus + behind)
    return 0


def mix_kernel(members, nx, own, from_low, from_high, after, onward, near, edges, token):
    token[...] = jnp.zeros_like(token)
    rate = ROOT_D**nx
    closure = 1.0 / (1.0 - rate**members)
    for k, came in enumerate((from_low, from_high)):
        onward[k] = own[k] + rate * came[1]
        near[k] = closure * (came[1] + rate ** (members - 1) * own[k])
        edges[k] = came[0]


def pair_kernel(nx, own, opposite, after, up, down, rest):
    rate = ROOT_F**nx
    closure = 1.0 / (1.0 - rate**4)
    up[...] = own[0] + rate**2 * opposite[0]
    down[...] = own[1] + rate**2 * opposite[1]
    rest[...] = (closure * rate) * opposite[...] + (closure * rate**3) * own[...]


def far_part(members, nx, x, across, v):
    rate = ROOT_D**nx
    closure = 1.0 / (1.0 - rate**members)
    low, high = across[0, v], across[1, v]
    return (closure * rate * ROOT_D ** (x + 1)) * low - (closure * rate * ROOT_D ** (nx - x)) * high


def register_kernel(members, new_inc, across, local, w_low, w_high, out_hbm, rim, out, sems):
    nx = new_inc.shape[1]
    for k in range(3):
        for v in range(5):
            rim[k, v] = local[v, k] - w_low[k, v]
            rim[5 - k, v] = local[v, nx - 1 - k] - w_high[k, v]
    done = []
    for v in range(5):
        for x in range(nx):
            e = far_part(members, nx, x, across, v)
            out[v, x] = new_inc[v, x] - (time_step * X["deriv"]) * e
        copy = pltpu.make_async_copy(out.at[v], out_hbm.at[v], sems.at[v])
        copy.start()
        done.append(copy)
    for copy in done:
        copy.wait()


def final_kernel(members, local, rim, across, incoming, out_hbm, out, sems):
    nx = local.shape[1]
    through = -section_b * time_step * X["deriv"] - X["slow"]
    done = []
    for v in range(5):
        low, high = incoming[0, v], incoming[1, v]
        for x in range(nx):
            value = local[v, x] if 3 <= x < nx - 3 else rim[x if x < 3 else x - nx + 6, v]
            value = value + through * far_part(members, nx, x, across, v)
            value = value - (ROOT_F ** (x + 1)) * low - (ROOT_F ** (nx - x)) * high
            out[v, x] = value
        copy = pltpu.make_async_copy(out.at[v], out_hbm.at[v], sems.at[v])
        copy.start()
        done.append(copy)
    for copy in done:
        copy.wait()


def shifted(value, axis, by):
    size = lax.axis_size(axis)
    return lax.ppermute(value, axis, [(i, (i + by) % size) for i in range(size)])


def ring_sums(own, rate):
    size = lax.axis_size("gx")
    gathered = lax.all_gather(own, "gx", axis=0)
    here = lax.axis_index("gx")
    member = jnp.arange(size, dtype=jnp.int32)
    table = jnp.asarray([rate**k / (1.0 - rate**size) for k in range(size)], f32)
    up = table[(here - 1 - member) % size]
    down = table[(member - here - 1) % size]
    shape = (size,) + (1,) * (own.ndim - 1)
    low = jnp.sum(up.reshape(shape) * gathered[:, 0], axis=0)
    high = jnp.sum(down.reshape(shape) * gathered[:, 1], axis=0)
    return jnp.stack([low, high])


def call(kernel, name, inputs, hbm, outputs, scratch):
    place = {True: pl.BlockSpec(memory_space=pltpu.HBM), False: pl.BlockSpec(memory_space=pltpu.VMEM)}
    shapes = [dims[1] if dims[0] == "hbm" else dims for dims in outputs]
    return pl.pallas_call(
        kernel,
        in_specs=[place[i < hbm] for i in range(len(inputs))],
        out_specs=[place[dims[0] == "hbm"] for dims in outputs],
        out_shape=[jax.ShapeDtypeStruct(dims, f32) for dims in shapes],
        scratch_shapes=scratch,
        compiler_params=pltpu.CompilerParams(vmem_limit_bytes=40 * 2**20),
        cost_estimate=pl.CostEstimate(flops=1000, bytes_accessed=1000, transcendentals=0),
        name=name,
    )(*[pltpu.with_memory_space_constraint(a, pltpu.HBM) if i < hbm else a for i, a in enumerate(inputs)])


def on_device(density, momentum, energy, increment):
    nx, ny, nz = density.shape
    members = lax.axis_size("gx")
    cells = nx * ny * nz
    state = (density, momentum, energy)
    face = (5, ny, nz)
    whole = (5, nx, ny, nz)

    def vmem(*dims):
        return pltpu.VMEM(dims, f32)

    def sems(*dims):
        return pltpu.SemaphoreType.DMA(dims)

    state_room = [vmem(nx, ny, nz), vmem(3, nx, ny, nz), vmem(nx, ny, nz)]

    up, down, own, g_rows, h_rows, z_up, z_down, z_own, y_edge, begun = call(
        face_kernel,
        "faces",
        state,
        3,
        [(2, *face), (2, *face), (2, *face), (8, *face), (8, *face), face, face, (2, *face), (5, nx + 2, 8, nz), (8, nz)],
        state_room + [sems(3, ny // 16)],
    )
    from_low = shifted(up, "gx", 1)
    from_high = shifted(down, "gx", -1)
    z_low = shifted(z_up, "gz", 1)
    z_high = shifted(z_down, "gz", -1)
    y_halo = shifted(y_edge, "gy", 1)

    base, w_up0, w_down0 = call(
        base_kernel,
        "base",
        (*state, increment, begun),
        4,
        [(2, *face), (3, *face), (3, *face)],
        state_room + [vmem(*whole), sems(4, ny // 16)],
    )
    table = jnp.asarray(fix_table(nz), jnp.bfloat16)
    sums, own_sums, w_up, w_down, fix = call(
        end_kernel,
        "ends",
        (base, w_up0, w_down0, g_rows, h_rows, y_halo, z_low, z_high, z_own, table),
        0,
        [(2, *face), (2, *face), (3, *face), (3, *face), (2, *face)],
        [vmem(8, 5, ny + 16, nz), vmem(8, *face)],
    )
    half = nx // 2
    half_room = [vmem(half, ny, nz), vmem(3, half, ny, nz), vmem(half, ny, nz), vmem(5, half, ny, nz)]
    part0, token = call(
        functools.partial(part_kernel, 0),
        "part0",
        (*state, increment, y_halo, fix),
        4,
        [(5, half, ny, nz), (8, nz)],
        half_room + [vmem(5, ny + 16, nz), sems(4, half // 4)],
    )
    onward, near, edges, mixed = call(
        functools.partial(mix_kernel, members, nx),
        "mix",
        (own, from_low, from_high, token),
        0,
        [(2, *face)] * 3 + [(8, nz)],
        [],
    )
    part1, token1 = call(
        functools.partial(part_kernel, half),
        "part1",
        (*state, increment, y_halo, fix, mixed),
        4,
        [(5, half, ny, nz), (8, nz)],
        half_room + [vmem(5, ny + 16, nz), sems(4, half // 4)],
    )

    rate_d, rate_f = ROOT_D**nx, ROOT_F**nx
    w_low = shifted(w_up, "gx", 1)
    w_high = shifted(w_down, "gx", -1)
    if members == 4:
        across = shifted(onward, "gx", 2)
        opposite = shifted(sums, "gx", 2)
        mixed_up, mixed_down, rest = call(
            functools.partial(pair_kernel, nx), "pair", (own_sums, opposite, token1), 0, [face, face, (2, *face)], []
        )
        beside = jnp.stack([shifted(mixed_up, "gx", 1), shifted(mixed_down, "gx", -1)])
        incoming = beside * (1.0 / (1.0 - rate_f**4)) + rest
    else:
        near = ring_sums(own, rate_d)
        across = jnp.zeros_like(near)
        incoming = ring_sums(sums, rate_f)

    new_local, local = call(
        line_kernel,
        "lines",
        (*state, edges, near, part0, part1),
        3,
        [whole, whole],
        state_room + [vmem(5, nx, 16, nz), vmem(5, nx, 16, nz), vmem(nx, 16, nz), sems(3, ny // 16)],
    )
    out_room = [vmem(*whole), sems(5)]
    new_increment, rim = call(
        functools.partial(register_kernel, members),
        "register",
        (new_local, across, local, w_low, w_high),
        0,
        [("hbm", whole), (6, *face)],
        out_room,
    )
    (new_state,) = call(
        functools.partial(final_kernel, members),
        "final",
        (local, rim, across, incoming),
        0,
        [("hbm", whole)],
        out_room,
    )
    return (new_state, new_increment)


def solution(mesh):
    in_specs = (
        P("gx", "gy", "gz"),
        P(None, "gx", "gy", "gz"),
        P("gx", "gy", "gz"),
        P(None, "gx", "gy", "gz"),
    )
    out_specs = (P(None, "gx", "gy", "gz"), P(None, "gx", "gy", "gz"))
    return jax.shard_map(
        on_device, mesh=mesh, in_specs=in_specs, out_specs=out_specs, check_vma=False
    )
```

```python
import functools
import math

import jax
import jax.numpy as jnp
import numpy as np
from jax import lax
from jax.experimental import pallas as pl
from jax.experimental.pallas import tpu as pltpu
from jax.sharding import PartitionSpec as P

deriv_alpha = 1.0 / 3.0
filter_alpha = 0.4999
gas_gamma = 1.4
time_step = 0.2
section_a = -5.0 / 9.0
section_b = 15.0 / 16.0
explicit_weights = (0.75, -0.15, 1.0 / 60.0)
f32 = jnp.float32


def root_of(coupling):
    return (-1.0 + math.sqrt(1.0 - 4.0 * coupling * coupling)) / (2.0 * coupling)


def laurent(poly, times_s):
    size = len(poly) + 1
    total = np.zeros(2 * size + 1)
    for power, value in enumerate(poly):
        term = np.array([1.0])
        for _ in range(power):
            term = np.convolve(term, [1.0, 0.0, 1.0])
        if times_s:
            term = np.convolve(term, [-1.0, 0.0, 1.0])
        half = len(term) // 2
        total[size - half : size + half + 1] += value * term
    return [float(v) for v in total[size:]]


def x_constants():
    ad, af = deriv_alpha, filter_alpha
    kappa = (1.0 / 36.0) / ad
    beta = 7.0 / 9.0 - kappa
    poly = np.polynomial.polynomial
    p_of_c = (1.0 - 2.0 * af) / 256.0 * poly.polypow([2.0, -1.0], 4)
    q_of_c, rest = poly.polydiv(p_of_c, [1.0, af])
    rho = float(rest[0])
    both = poly.polymul([1.0, af], [1.0, ad])
    q2_of_c, _ = poly.polydiv(p_of_c, both)
    mu_f = float(poly.polyval(-1.0 / af, p_of_c)) / (1.0 - ad / af)
    mu_d = float(poly.polyval(-1.0 / ad, p_of_c)) / (1.0 - af / ad)
    b_of_c = poly.polyadd(kappa * q_of_c, beta * q2_of_c)
    g = 1.0 / math.sqrt(1.0 - 4.0 * af * af)
    sigma = -section_b * time_step
    return dict(
        kappa=kappa,
        deriv=beta / ad,
        band_q=laurent(q_of_c, False)[:4],
        band_f=[sigma * v for v in laurent(b_of_c, True)[:5]],
        own=rho * g,
        pair=sigma * (kappa * rho + beta * mu_f) / af,
        slow=sigma * beta * mu_d / ad,
    )


X = x_constants()
ROOT_D = root_of(deriv_alpha)
ROOT_F = root_of(filter_alpha)


def primitives(cells):
    density, m0, m1, m2, energy = cells
    inverse = 1.0 / density
    squared = m0 * m0 + m1 * m1 + m2 * m2
    pressure = (gas_gamma - 1.0) * (energy - 0.5 * squared * inverse)
    return inverse, pressure


def flux(cells, inverse, pressure, axis_k):
    momentum = cells[1:4]
    velocity = momentum[axis_k] * inverse
    parts = [
        momentum[axis_k],
        momentum[0] * velocity,
        momentum[1] * velocity,
        momentum[2] * velocity,
        (cells[4] + pressure) * velocity,
    ]
    parts[axis_k + 1] = parts[axis_k + 1] + pressure
    return parts


def lanes(shape):
    return lax.broadcasted_iota(jnp.int32, shape, len(shape) - 1)


def roll(value, amount):
    size = value.shape[-1]
    if isinstance(amount, int):
        amount = amount % size
        if amount == 0:
            return value
    return pltpu.roll(value, amount, value.ndim - 1)


class Blocks:
    def __init__(self, sources, targets, sems, dims, size, begin=0):
        self.parts = list(zip(sources, targets, dims, strict=True))
        self.sems, self.size, self.begin = sems, size, begin
        self.count = targets[0].shape[dims[0]] // size

        def start(k, _):
            for copy in self.piece(k):
                copy.start()
            return 0

        lax.fori_loop(0, self.count, start, 0)

    def piece(self, k):
        copies = []
        for n, (source, target, dim) in enumerate(self.parts):
            lead = (slice(None),) * dim
            first = pl.multiple_of(k * self.size, self.size)
            there = source.at[(*lead, pl.ds(self.begin + first, self.size))]
            here = target.at[(*lead, pl.ds(first, self.size))]
            copies.append(pltpu.make_async_copy(there, here, self.sems.at[n, k]))
        return copies

    def wait(self, k):
        for copy in self.piece(k):
            copy.wait()

    def each(self, body, steps):
        def one(k, _):
            self.wait(k)
            lax.fori_loop(k * steps, (k + 1) * steps, body, 0)
            return 0

        lax.fori_loop(0, self.count, one, 0)


def write_out(kernel_part, pieces, copy_of):
    def one(k, _):
        kernel_part(k)
        copy_of(k).start()
        return 0

    def wait(k, _):
        copy_of(k).wait()
        return 0

    lax.fori_loop(0, pieces, one, 0)
    lax.fori_loop(0, pieces, wait, 0)


def cells_at(rho, mom, ene, x, at):
    return [rho[x, at], mom[0, x, at], mom[1, x, at], mom[2, x, at], ene[x, at]]


def face_kernel(
    rho_hbm, mom_hbm, ene_hbm,
    to_partner, to_other, own, g_rows, h_rows, z_up, z_down, z_own, y_edge, token,
    rho, mom, ene, sems,
):
    nx, ny, nz = rho.shape
    lane = lanes((8, nz))
    slot = lane // 8
    first_half = lane % 8 < 4
    row = lax.broadcasted_iota(jnp.int32, (8, nz), 0)
    stored = {x: r for r, x in enumerate((0, 1, 2, nx - 3, nx - 2, nx - 1))}
    rows = 16
    blocks = Blocks((rho_hbm, mom_hbm, ene_hbm), (rho, mom, ene), sems, (1, 2, 1), rows)
    token[...] = jnp.zeros_like(token)
    odd = is_upper()

    def tile(t, _):
        at = pl.ds(pl.multiple_of(8 * t, 8), 8)
        keep = (row < 4) & (t > 0)
        packed = [[None] * 5, [None] * 5]
        totals = lower = upper = None
        for x in range(nx):
            cells = cells_at(rho, mom, ene, x, at)
            inverse, pressure = primitives(cells)
            f = flux(cells, inverse, pressure, 0)
            g = flux(cells, inverse, pressure, 1)
            h = flux(cells, inverse, pressure, 2)
            group, place = x // 16, x % 16
            for v in range(5):
                y_edge[v, x] = jnp.where(keep, y_edge[v, x], g[v])
                moved = roll(cells[v], 8 * place + 3)
                if place:
                    moved = jnp.where(slot == place, moved, packed[group][v])
                packed[group][v] = moved
                if x in stored:
                    g_rows[stored[x], v, at] = g[v]
                    h_rows[stored[x], v, at] = h[v]
                if x == 0:
                    to_other[v, at] = f[v]
                if x == nx - 1:
                    first = to_other[v, at]
                    to_partner[2, v, at] = jnp.where(odd, first, f[v])
                    to_other[v, at] = jnp.where(odd, f[v], first)
            if x == 0:
                totals, lower, upper = [g, h, g, h], f, f
            else:
                lower = [ROOT_D * a + b for a, b in zip(lower, f)]
                upper = [a + ROOT_D**x * b for a, b in zip(upper, f)]
                factor = ROOT_F**x
                totals = [
                    [ROOT_F * a + b if k < 2 else a + factor * b for a, b in zip(total, term)]
                    for k, (total, term) in enumerate(zip(totals, (g, h, g, h)))
                ]
        h = [flux(packed[group], *primitives(packed[group]), 2) for group in range(2)]
        for v in range(5):
            to_partner[0, v, at] = own[0, v, at] = lower[v]
            to_partner[1, v, at] = own[1, v, at] = upper[v]
            for k in range(2):
                g_rows[6 + k, v, at] = totals[2 * k][v]
                h_rows[6 + k, v, at] = totals[2 * k + 1][v]
                y_edge[v, nx + k] = jnp.where(keep, y_edge[v, nx + k], totals[2 * k][v])
                group, place = (nx + k) // 16, (nx + k) % 16
                moved = roll(totals[2 * k + 1][v], 8 * place + 3)
                h[group][v] = jnp.where(slot == place, moved, h[group][v])
            for group in range(2):
                z_own[group, v, at] = h[group][v]
            z_up[v, at] = jnp.where(first_half, h[0][v], roll(h[1][v], 4))
            z_down[v, at] = jnp.where(first_half, roll(h[0][v], -3), roll(h[1][v], 1))
        return 0

    blocks.each(tile, rows // 8)


def base_kernel(rho_hbm, mom_hbm, ene_hbm, inc_hbm, after, base, w_up, w_down, rho, mom, ene, inc, sems):
    nx, ny, nz = rho.shape
    rows = 16
    blocks = Blocks((rho_hbm, mom_hbm, ene_hbm, inc_hbm), (rho, mom, ene, inc), sems, (1, 2, 1, 2), rows)

    def tile(t, _):
        at = pl.ds(pl.multiple_of(8 * t, 8), 8)
        totals = None
        ends = {1.0: [[None] * 5 for _ in range(3)], -1.0: [[None] * 5 for _ in range(3)]}
        for x in range(nx):
            cells = cells_at(rho, mom, ene, x, at)
            f = flux(cells, *primitives(cells), 0)
            q = [cells[v] + (section_a * section_b) * inc[v, x, at] for v in range(5)]
            own = [X["own"] * q[v] for v in range(5)]
            pair = [X["pair"] * f[v] for v in range(5)]
            plus = [a + b for a, b in zip(own, pair)]
            minus = [a - b for a, b in zip(own, pair)]
            if x == 0:
                totals = [plus, minus]
            else:
                totals[0] = [ROOT_F * a + b for a, b in zip(totals[0], plus)]
                totals[1] = [a + ROOT_F**x * b for a, b in zip(totals[1], minus)]
            for sign, j in ((1.0, x + 1), (-1.0, nx - x)):
                for k in range(3):
                    n = k + j
                    if n > 4:
                        continue
                    for v in range(5):
                        term = (sign * X["band_f"][n]) * f[v]
                        if n <= 3:
                            term = term + X["band_q"][n] * q[v]
                        so_far = ends[sign][k][v]
                        ends[sign][k][v] = term if so_far is None else so_far + term
            if x == 3:
                for k in range(3):
                    for v in range(5):
                        w_down[k, v, at] = ends[1.0][k][v]
        for v in range(5):
            base[0, v, at] = totals[0][v]
            base[1, v, at] = totals[1][v]
            for k in range(3):
                w_up[k, v, at] = ends[-1.0][k][v]
        return 0

    blocks.each(tile, rows // 8)


def fix_table(nz):
    weight = {1: 45.0, 2: -9.0, 3: 1.0}
    table = np.zeros((4 * nz, 2 * nz))
    for group in range(2):
        for place in range(nz // 8):
            into = group * nz + 8 * place
            came = 8 * place + 4 * group
            kept = (2 + group) * nz + 8 * place
            for j in range(3):
                for n, w in weight.items():
                    if j + n >= 3:
                        table[nz + came + j + n - 3, into + j] += w
                        table[kept + 3 + j + n - 3, into + j] -= w
                    if n > j:
                        table[came + 3 + j - n, into + 3 + j] -= w
                        table[kept + 3 + j - n, into + 3 + j] += w
    return table


def split(value):
    high = value.astype(jnp.bfloat16)
    return high, (value - high.astype(f32)).astype(jnp.bfloat16)


def around(at):
    return 45.0 * (at(1) - at(-1)) - 9.0 * (at(2) - at(-2)) + (at(3) - at(-3))


def along_lanes(h):
    v1 = roll(h, -1)
    v2 = roll(v1 - 9.0 * h, -2)
    both = 9.0 * v1 - h
    return 5.0 * both + v2 + roll(both + 5.0 * v2, 3)


def turn_of(x, nz):
    if isinstance(x, int):
        return (2 * nz - 3 - 8 * (x % 16)) % nz
    return lax.rem(2 * nz - 3 - 8 * lax.rem(x, 16), nz)


def end_kernel(
    base, w_up0, w_down0, g_rows, h_rows, y_halo, z_low, z_high, z_own, table,
    sums, own_sums, to_other, to_partner, fix, token, pad, dz_all,
):
    token[...] = jnp.zeros_like(token)
    ny, nz = base.shape[2:]
    nx = y_halo.shape[1] - 2
    lane = lanes((8, nz))
    edge_lane = (lane < 3) | (lane >= nz - 3)
    parts = [z_low[...], z_high[...], z_own[0], z_own[1]]
    halves = [split(p.reshape(5 * ny, nz)) for p in parts]
    fixed = sum(
        jnp.dot(jnp.concatenate([h[k] for h in halves], axis=1), table[...], preferred_element_type=f32)
        for k in range(2)
    )
    for group in range(2):
        fix[group] = fixed[:, group * nz : group * nz + nz].reshape(5, ny, nz)
    rows = [0, 1, 2, nx - 3, nx - 2, nx - 1, nx, nx + 1]
    for r, x in enumerate(rows):
        for v in range(5):
            pad[r, v, 0:8] = y_halo[v, x]
            pad[r, v, ny + 8 : ny + 16] = y_halo[v, x]

    def first(t, _):
        at = pl.ds(pl.multiple_of(8 * t, 8), 8)
        inside = pl.ds(pl.multiple_of(8 * t + 8, 8), 8)
        for r, x in enumerate(rows):
            for v in range(5):
                h = h_rows[r, v, at]
                pad[r, v, inside] = g_rows[r, v, at]
                moved = roll(fix[x // 16, v, at], turn_of(x, nz))
                dz_all[r, v, at] = along_lanes(h) + jnp.where(edge_lane, moved, 0.0)
        return 0

    lax.fori_loop(0, ny // 8, first, 0)
    scale = -time_step * section_b / 60.0

    odd = is_upper()

    def second(v, _):
        for t in range(ny // 8):
            at = slice(8 * t, 8 * t + 8)

            def cross(r, t=t, at=at):
                dy = around(lambda n: pad[r, v, 8 + 8 * t + n : 16 + 8 * t + n])
                return scale * (dy + dz_all[r, v, at])

            for k in range(2):
                sums[k, v, at] = own_sums[k, v, at] = base[k, v, at] + X["own"] * cross(6 + k)
            faces = []
            for begin, near in ((w_down0, (0, 1, 2)), (w_up0, (5, 4, 3))):
                q = [cross(r) for r in near]
                for k in range(3):
                    total = begin[k, v, at]
                    for j in range(1, 4 - k):
                        total = total + X["band_q"][k + j] * q[j - 1]
                    faces.append(total)
            for k in range(3):
                to_other[k, v, at] = jnp.where(odd, faces[3 + k], faces[k])
                to_partner[k, v, at] = jnp.where(odd, faces[k], faces[3 + k])
        return 0

    lax.fori_loop(0, 5, second, 0)


def part_kernel(
    rho_hbm, mom_hbm, ene_hbm, inc_hbm, y_halo, fix, after,
    part, token,
    rho, mom, ene, inc, pad, sems,
):
    token[...] = jnp.zeros_like(token)
    nx, ny, nz = rho.shape
    lane = lanes((8, nz))
    edge_lane = (lane < 3) | (lane >= nz - 3)
    scale = -time_step / 60.0
    some = 4
    blocks = Blocks((rho_hbm, mom_hbm, ene_hbm, inc_hbm), (rho, mom, ene, inc), sems, (0, 1, 0, 1), some)

    def one_row(x, _):
        turn = turn_of(x, nz)
        group = x // 16
        for v in range(5):
            pad[v, 0:8] = y_halo[v, x]
            pad[v, ny + 8 : ny + 16] = y_halo[v, x]
        for t in range(ny // 8):
            at = slice(8 * t, 8 * t + 8)
            cells = cells_at(rho, mom, ene, x, at)
            inverse, pressure = primitives(cells)
            g = flux(cells, inverse, pressure, 1)
            h = flux(cells, inverse, pressure, 2)
            for v in range(5):
                pad[v, 8 + 8 * t : 16 + 8 * t] = g[v]
                dz = along_lanes(h[v])
                dz = dz + jnp.where(edge_lane, roll(fix[group, v, at], turn), 0.0)
                part[v, x, at] = section_a * inc[v, x, at] + scale * dz
        for t in range(ny // 8):
            at = slice(8 * t, 8 * t + 8)
            for v in range(5):
                dy = around(lambda n, v=v, t=t: pad[v, 8 + 8 * t + n : 16 + 8 * t + n])
                part[v, x, at] = part[v, x, at] + scale * dy
        return 0

    blocks.each(one_row, some)


def line_kernel(rho_hbm, mom_hbm, ene_hbm, f_low, f_high, part, *rest):
    *sums, new_inc_hbm, local = rest[:-9]
    rho, mom, ene, new_inc, f_all, q_all, e_all, sems, out_sems = rest[-9:]
    nx, ny, nz = rho.shape
    rows = 16
    blocks = Blocks((rho_hbm, mom_hbm, ene_hbm), (rho, mom, ene), sems, (1, 2, 1), rows)

    def copy_of(k):
        at = pl.ds(pl.multiple_of(k * rows, rows), rows)
        return pltpu.make_async_copy(new_inc.at[:, :, at], new_inc_hbm.at[:, :, at], out_sems.at[k])

    def slab(k):
        blocks.wait(k)
        at = pl.ds(pl.multiple_of(k * rows, rows), rows)

        def fluxes_at(x, _):
            cells = cells_at(rho, mom, ene, x, at)
            for v, value in enumerate(flux(cells, *primitives(cells), 0)):
                f_all[v, x] = value
                q_all[v, x] = cells[v] + section_b * part[v, x, at]
            return 0

        lax.fori_loop(0, nx, fluxes_at, 0)
        lines_of = functools.partial(one_line, at, part, f_low, f_high, sums, new_inc, local, f_all, q_all, e_all)
        lax.fori_loop(0, 5, lines_of, 0)

    write_out(slab, ny // rows, copy_of)


def one_line(at, part, f_low, f_high, sums, new_inc, local, f_all, q_all, e_all, v, _):
    nx = f_all.shape[1]
    f = [f_all[v, x] for x in range(nx)]
    q = [q_all[v, x] for x in range(nx)]
    low, high = f_low[v, at], f_high[v, at]
    from_low, from_high = incoming(ROOT_D**nx, sums, v, at)
    forward = ROOT_D * from_low
    for x in range(nx):
        e_all[x] = forward
        forward = ROOT_D * (f[x] + forward)
    backward = ROOT_D * from_high
    for x in reversed(range(nx)):
        e_all[x] = e_all[x] - backward
        backward = ROOT_D * (f[x] + backward)
    ahead = None
    for x in range(nx):
        before = low if x == 0 else f[x - 1]
        after = high if x == nx - 1 else f[x + 1]
        e = e_all[x]
        deriv = X["kappa"] * (after - before) + X["deriv"] * e
        new_inc[v, x, at] = part[v, x, at] - time_step * deriv
        total = (1.0 - X["band_q"][0] - X["own"]) * q[x] - X["slow"] * e
        total = total - (section_b * time_step) * deriv
        for n in range(1, 4):
            near = [q[i] for i in (x - n, x + n) if 0 <= i < nx]
            total = total - X["band_q"][n] * (near[0] if len(near) == 1 else near[0] + near[1])
        for n in range(1, 5):
            if x + n < nx and x - n >= 0:
                total = total - X["band_f"][n] * (f[x + n] - f[x - n])
            elif x + n < nx:
                total = total - X["band_f"][n] * f[x + n]
            else:
                total = total + X["band_f"][n] * f[x - n]
        if x == 3:
            total = total + X["band_f"][4] * low
        if x == nx - 4:
            total = total - X["band_f"][4] * high
        if ahead is not None:
            total = total - ahead
        local[v, x, at] = total
        plus = X["own"] * q[x] + X["pair"] * f[x]
        ahead = ROOT_F * (plus if ahead is None else plus + ahead)
    behind = None
    for x in reversed(range(nx)):
        if behind is not None:
            local[v, x, at] = local[v, x, at] - behind
        minus = X["own"] * q[x] - X["pair"] * f[x]
        behind = ROOT_F * (minus if behind is None else minus + behind)
    return 0


def is_upper():
    return lax.axis_index("gx") % 2 == 1


def incoming(rate, sums, v, at):
    if len(sums) == 1:
        return sums[0][0, v, at], sums[0][1, v, at]
    beside, pair, opposite = sums
    closure = 1.0 / (1.0 - rate**4)
    low, high = (closure * (opposite[k, v, at] + rate**2 * pair[k, v, at]) for k in range(2))
    odd = is_upper()
    return (
        jnp.where(odd, beside[0, v, at] + rate * low, low),
        jnp.where(odd, high, beside[1, v, at] + rate * high),
    )


def mix_kernel(rate, own, came, after, *rest):
    *others, out, pair, beside, token = rest
    odd = is_upper()
    token[...] = jnp.zeros_like(token)
    for v in range(5):
        upper = jnp.where(odd, own[0, v] + rate * came[0, v], came[0, v] + rate * own[0, v])
        lower = jnp.where(odd, came[1, v] + rate * own[1, v], own[1, v] + rate * came[1, v])
        out[0, v] = pair[0, v] = upper
        out[1, v] = pair[1, v] = lower
        if len(others) == 5:
            w_taken, f_taken, f_near, w_given, f_given = others
            f_near[v] = came[2, v]
            f_given[v] = f_taken[v]
            for k in range(3):
                w_given[k, v] = w_taken[k, v]
        else:
            near, other, low, high = others
            low[v] = jnp.where(odd, near[v], other[v])
            high[v] = jnp.where(odd, other[v], near[v])
    beside[0] = came[0]
    beside[1] = came[1]


def final_kernel(local, w_other, w_partner, *rest):
    odd = is_upper()
    *sums, out_hbm, out, sems = rest
    nx = local.shape[1]

    def one(v):
        low, high = incoming(ROOT_F**nx, sums, v, slice(None))
        for x in range(nx):
            value = local[v, x] - (ROOT_F ** (x + 1)) * low - (ROOT_F ** (nx - x)) * high
            if x < 3:
                value = value - jnp.where(odd, w_partner[x, v], w_other[x, v])
            if x >= nx - 3:
                value = value - jnp.where(odd, w_other[nx - 1 - x, v], w_partner[nx - 1 - x, v])
            out[v, x] = value

    write_out(one, 5, lambda v: pltpu.make_async_copy(out.at[v], out_hbm.at[v], sems.at[v]))


def shifted(value, axis, by):
    size = lax.axis_size(axis)
    return lax.ppermute(value, axis, [(i, (i + by) % size) for i in range(size)])


def ring_sums(own, rate):
    size = lax.axis_size("gx")
    gathered = lax.all_gather(own, "gx", axis=0)
    here = lax.axis_index("gx")
    member = jnp.arange(size, dtype=jnp.int32)
    table = jnp.asarray([rate**k / (1.0 - rate**size) for k in range(size)], f32)
    up = table[(here - 1 - member) % size]
    down = table[(member - here - 1) % size]
    shape = (size,) + (1,) * (own.ndim - 1)
    low = jnp.sum(up.reshape(shape) * gathered[:, 0], axis=0)
    high = jnp.sum(down.reshape(shape) * gathered[:, 1], axis=0)
    return jnp.stack([low, high])


def call(kernel, name, inputs, hbm, outputs, scratch):
    place = {True: pl.BlockSpec(memory_space=pltpu.HBM), False: pl.BlockSpec(memory_space=pltpu.VMEM)}
    shapes = [dims[1] if dims[0] == "hbm" else dims for dims in outputs]
    return pl.pallas_call(
        kernel,
        in_specs=[place[i < hbm] for i in range(len(inputs))],
        out_specs=[place[dims[0] == "hbm"] for dims in outputs],
        out_shape=[jax.ShapeDtypeStruct(dims, f32) for dims in shapes],
        scratch_shapes=scratch,
        compiler_params=pltpu.CompilerParams(vmem_limit_bytes=40 * 2**20),
        cost_estimate=pl.CostEstimate(flops=1000, bytes_accessed=1000, transcendentals=0),
        name=name,
    )(*[pltpu.with_memory_space_constraint(a, pltpu.HBM) if i < hbm else a for i, a in enumerate(inputs)])


def on_device(density, momentum, energy, increment):
    nx, ny, nz = density.shape
    members = lax.axis_size("gx")
    cells = nx * ny * nz
    state = (density, momentum, energy)
    face = (5, ny, nz)
    whole = (5, nx, ny, nz)

    def vmem(*dims):
        return pltpu.VMEM(dims, f32)

    def sems(*dims):
        return pltpu.SemaphoreType.DMA(dims)

    state_room = [vmem(nx, ny, nz), vmem(3, nx, ny, nz), vmem(nx, ny, nz)]

    to_partner, to_other, own_d, g_rows, h_rows, z_up, z_down, z_own, y_edge, begun = call(
        face_kernel,
        "faces",
        state,
        3,
        [(3, *face), face, (2, *face), (8, *face), (8, *face), face, face, (2, *face), (5, nx + 2, 8, nz), (8, nz)],
        state_room + [sems(3, ny // 16)],
    )
    z_low = shifted(z_up, "gz", 1)
    z_high = shifted(z_down, "gz", -1)
    y_halo = shifted(y_edge, "gy", 1)

    base, w_up0, w_down0 = call(
        base_kernel,
        "base",
        (*state, increment, begun),
        4,
        [(2, *face), (3, *face), (3, *face)],
        state_room + [vmem(*whole), sems(4, ny // 16)],
    )
    table = jnp.asarray(fix_table(nz), jnp.bfloat16)
    sums, own_sums, w_to_other, w_to_partner, fix, ended = call(
        end_kernel,
        "ends",
        (base, w_up0, w_down0, g_rows, h_rows, y_halo, z_low, z_high, z_own, table),
        0,
        [(2, *face), (2, *face), (3, *face), (3, *face), (2, *face), (8, nz)],
        [vmem(8, 5, ny + 16, nz), vmem(8, *face)],
    )
    rate_d, rate_f = ROOT_D**nx, ROOT_F**nx
    token = ended
    if members == 4:
        partner = [(i, i ^ 1) for i in range(members)]
        other = [(i, (i + 1 - 2 * (i % 2 == 0)) % members) for i in range(members)]
        mixed = [(2, *face)] * 3 + [(8, nz)]
        d_came = lax.ppermute(to_partner, "gx", partner)
        f_came = lax.ppermute(sums, "gx", partner)
        w_partner = lax.ppermute(w_to_partner, "gx", partner)
        f_near, w_to_other, to_other, group, d_pair, d_beside, token = call(
            functools.partial(mix_kernel, rate_d),
            "mixd",
            (own_d, d_came, ended, w_to_other, to_other),
            0,
            [face, (3, *face), face] + mixed,
            [],
        )
        f_other = lax.ppermute(to_other, "gx", other)
        w_other = lax.ppermute(w_to_other, "gx", other)
        far = (d_beside, d_pair, shifted(group, "gx", 2))
    else:
        odd = lax.axis_index("gx") % 2 == 1
        f_low = shifted(jnp.where(odd, to_other, to_partner[2]), "gx", 1)
        f_high = shifted(jnp.where(odd, to_partner[2], to_other), "gx", -1)
        far = (ring_sums(own_d, rate_d),)
        w_low = shifted(jnp.where(odd, w_to_other, w_to_partner), "gx", 1)
        w_high = shifted(jnp.where(odd, w_to_partner, w_to_other), "gx", -1)
        w_other, w_partner = jnp.where(odd, w_high, w_low), jnp.where(odd, w_low, w_high)
    part, parted = call(
        part_kernel,
        "part",
        (*state, increment, y_halo, fix, token),
        4,
        [whole, (8, nz)],
        state_room + [vmem(*whole), vmem(5, ny + 16, nz), sems(4, nx // 4)],
    )
    if members == 4:
        f_low, f_high, group, f_pair, f_beside, _ = call(
            functools.partial(mix_kernel, rate_f),
            "mixf",
            (own_sums, f_came, parted, f_near, f_other),
            0,
            [face, face] + mixed,
            [],
        )
        from_others = (f_beside, f_pair, shifted(group, "gx", 2))
    else:
        from_others = (ring_sums(own_sums, rate_f),)
    new_increment, local = call(
        line_kernel,
        "lines",
        (*state, f_low, f_high, part, *far),
        3,
        [("hbm", whole), whole],
        state_room
        + [vmem(*whole), vmem(5, nx, 16, nz), vmem(5, nx, 16, nz), vmem(nx, 16, nz)]
        + [sems(3, ny // 16), sems(ny // 16)],
    )
    (new_state,) = call(
        final_kernel,
        "final",
        (local, w_other, w_partner, *from_others),
        0,
        [("hbm", whole)],
        [vmem(*whole), sems(5)],
    )
    return (new_state, new_increment)


def solution(mesh):
    in_specs = (
        P("gx", "gy", "gz"),
        P(None, "gx", "gy", "gz"),
        P("gx", "gy", "gz"),
        P(None, "gx", "gy", "gz"),
    )
    out_specs = (P(None, "gx", "gy", "gz"), P(None, "gx", "gy", "gz"))
    return jax.shard_map(
        on_device, mesh=mesh, in_specs=in_specs, out_specs=out_specs, check_vma=False
    )
```

```python
import functools
import math

import jax
import jax.numpy as jnp
import numpy as np
from jax import lax
from jax.experimental import pallas as pl
from jax.experimental.pallas import tpu as pltpu
from jax.sharding import PartitionSpec as P

deriv_alpha = 1.0 / 3.0
filter_alpha = 0.4999
gas_gamma = 1.4
time_step = 0.2
section_a = -5.0 / 9.0
section_b = 15.0 / 16.0
explicit_weights = (0.75, -0.15, 1.0 / 60.0)
f32 = jnp.float32
FIRST_ROWS = 12


def root_of(coupling):
    return (-1.0 + math.sqrt(1.0 - 4.0 * coupling * coupling)) / (2.0 * coupling)


def laurent(poly, times_s):
    size = len(poly) + 1
    total = np.zeros(2 * size + 1)
    for power, value in enumerate(poly):
        term = np.array([1.0])
        for _ in range(power):
            term = np.convolve(term, [1.0, 0.0, 1.0])
        if times_s:
            term = np.convolve(term, [-1.0, 0.0, 1.0])
        half = len(term) // 2
        total[size - half : size + half + 1] += value * term
    return [float(v) for v in total[size:]]


def x_constants():
    ad, af = deriv_alpha, filter_alpha
    kappa = (1.0 / 36.0) / ad
    beta = 7.0 / 9.0 - kappa
    poly = np.polynomial.polynomial
    p_of_c = (1.0 - 2.0 * af) / 256.0 * poly.polypow([2.0, -1.0], 4)
    q_of_c, rest = poly.polydiv(p_of_c, [1.0, af])
    rho = float(rest[0])
    both = poly.polymul([1.0, af], [1.0, ad])
    q2_of_c, _ = poly.polydiv(p_of_c, both)
    mu_f = float(poly.polyval(-1.0 / af, p_of_c)) / (1.0 - ad / af)
    mu_d = float(poly.polyval(-1.0 / ad, p_of_c)) / (1.0 - af / ad)
    b_of_c = poly.polyadd(kappa * q_of_c, beta * q2_of_c)
    g = 1.0 / math.sqrt(1.0 - 4.0 * af * af)
    sigma = -section_b * time_step
    return dict(
        kappa=kappa,
        deriv=beta / ad,
        band_q=laurent(q_of_c, False)[:4],
        band_f=[sigma * v for v in laurent(b_of_c, True)[:5]],
        own=rho * g,
        pair=sigma * (kappa * rho + beta * mu_f) / af,
        slow=sigma * beta * mu_d / ad,
    )


X = x_constants()
ROOT_D = root_of(deriv_alpha)
ROOT_F = root_of(filter_alpha)


def primitives(cells):
    density, m0, m1, m2, energy = cells
    inverse = 1.0 / density
    squared = m0 * m0 + m1 * m1 + m2 * m2
    pressure = (gas_gamma - 1.0) * (energy - 0.5 * squared * inverse)
    return inverse, pressure


def flux(cells, inverse, pressure, axis_k):
    momentum = cells[1:4]
    velocity = momentum[axis_k] * inverse
    parts = [
        momentum[axis_k],
        momentum[0] * velocity,
        momentum[1] * velocity,
        momentum[2] * velocity,
        (cells[4] + pressure) * velocity,
    ]
    parts[axis_k + 1] = parts[axis_k + 1] + pressure
    return parts


def lanes(shape):
    return lax.broadcasted_iota(jnp.int32, shape, len(shape) - 1)


def roll(value, amount):
    size = value.shape[-1]
    if isinstance(amount, int):
        amount = amount % size
        if amount == 0:
            return value
    return pltpu.roll(value, amount, value.ndim - 1)


class Blocks:
    def __init__(self, sources, targets, sems, dims, size, begin=0):
        self.parts = list(zip(sources, targets, dims, strict=True))
        self.sems, self.size, self.begin = sems, size, begin
        self.count = targets[0].shape[dims[0]] // size

        def start(k, _):
            for copy in self.piece(k):
                copy.start()
            return 0

        lax.fori_loop(0, self.count, start, 0)

    def piece(self, k):
        copies = []
        for n, (source, target, dim) in enumerate(self.parts):
            lead = (slice(None),) * dim
            first = pl.multiple_of(k * self.size, self.size)
            there = source.at[(*lead, pl.ds(self.begin + first, self.size))]
            here = target.at[(*lead, pl.ds(first, self.size))]
            copies.append(pltpu.make_async_copy(there, here, self.sems.at[n, k]))
        return copies

    def wait(self, k):
        for copy in self.piece(k):
            copy.wait()

    def each(self, body, steps):
        def one(k, _):
            self.wait(k)
            lax.fori_loop(k * steps, (k + 1) * steps, body, 0)
            return 0

        lax.fori_loop(0, self.count, one, 0)


def write_out(kernel_part, pieces, copy_of):
    def one(k, _):
        kernel_part(k)
        copy_of(k).start()
        return 0

    def wait(k, _):
        copy_of(k).wait()
        return 0

    lax.fori_loop(0, pieces, one, 0)
    lax.fori_loop(0, pieces, wait, 0)


def cells_at(rho, mom, ene, x, at):
    return [rho[x, at], mom[0, x, at], mom[1, x, at], mom[2, x, at], ene[x, at]]


def face_kernel(
    rho_hbm, mom_hbm, ene_hbm,
    to_partner, own, g_rows, h_rows, z_up, z_down, z_own, y_edge, token,
    rho, mom, ene, sems,
):
    nx, ny, nz = rho.shape
    lane = lanes((8, nz))
    slot = lane // 8
    first_half = lane % 8 < 4
    row = lax.broadcasted_iota(jnp.int32, (8, nz), 0)
    stored = {x: r for r, x in enumerate((0, 1, 2, nx - 3, nx - 2, nx - 1))}
    rows = 16
    blocks = Blocks((rho_hbm, mom_hbm, ene_hbm), (rho, mom, ene), sems, (1, 2, 1), rows)
    token[...] = jnp.zeros_like(token)
    odd = is_upper()

    def tile(t, _):
        at = pl.ds(pl.multiple_of(8 * t, 8), 8)
        keep = (row < 4) & (t > 0)
        packed = [[None] * 5, [None] * 5]
        totals = lower = upper = None
        for x in range(nx):
            cells = cells_at(rho, mom, ene, x, at)
            inverse, pressure = primitives(cells)
            f = flux(cells, inverse, pressure, 0)
            g = flux(cells, inverse, pressure, 1)
            h = flux(cells, inverse, pressure, 2)
            group, place = x // 16, x % 16
            for v in range(5):
                y_edge[v, x] = jnp.where(keep, y_edge[v, x], g[v])
                moved = roll(cells[v], 8 * place + 3)
                if place:
                    moved = jnp.where(slot == place, moved, packed[group][v])
                packed[group][v] = moved
                if x in stored:
                    g_rows[stored[x], v, at] = g[v]
                    h_rows[stored[x], v, at] = h[v]
                if x == 0:
                    to_partner[2, v, at] = f[v]
                if x == nx - 1:
                    first = to_partner[2, v, at]
                    to_partner[2, v, at] = jnp.where(odd, first, f[v])
                    to_partner[3, v, at] = jnp.where(odd, f[v], first)
            if x == 0:
                totals, lower, upper = [g, h, g, h], f, f
            else:
                lower = [ROOT_D * a + b for a, b in zip(lower, f)]
                upper = [a + ROOT_D**x * b for a, b in zip(upper, f)]
                factor = ROOT_F**x
                totals = [
                    [ROOT_F * a + b if k < 2 else a + factor * b for a, b in zip(total, term)]
                    for k, (total, term) in enumerate(zip(totals, (g, h, g, h)))
                ]
        h = [flux(packed[group], *primitives(packed[group]), 2) for group in range(2)]
        for v in range(5):
            to_partner[0, v, at] = own[0, v, at] = lower[v]
            to_partner[1, v, at] = own[1, v, at] = upper[v]
            for k in range(2):
                g_rows[6 + k, v, at] = totals[2 * k][v]
                h_rows[6 + k, v, at] = totals[2 * k + 1][v]
                y_edge[v, nx + k] = jnp.where(keep, y_edge[v, nx + k], totals[2 * k][v])
                group, place = (nx + k) // 16, (nx + k) % 16
                moved = roll(totals[2 * k + 1][v], 8 * place + 3)
                h[group][v] = jnp.where(slot == place, moved, h[group][v])
            for group in range(2):
                z_own[group, v, at] = h[group][v]
            z_up[v, at] = jnp.where(first_half, h[0][v], roll(h[1][v], 4))
            z_down[v, at] = jnp.where(first_half, roll(h[0][v], -3), roll(h[1][v], 1))
        return 0

    blocks.each(tile, rows // 8)


def base_kernel(rho_hbm, mom_hbm, ene_hbm, inc_hbm, after, base, w_up, w_down, rho, mom, ene, inc, sems):
    nx, ny, nz = rho.shape
    rows = 16
    blocks = Blocks((rho_hbm, mom_hbm, ene_hbm, inc_hbm), (rho, mom, ene, inc), sems, (1, 2, 1, 2), rows)

    def tile(t, _):
        at = pl.ds(pl.multiple_of(8 * t, 8), 8)
        totals = None
        ends = {1.0: [[None] * 5 for _ in range(3)], -1.0: [[None] * 5 for _ in range(3)]}
        for x in range(nx):
            cells = cells_at(rho, mom, ene, x, at)
            f = flux(cells, *primitives(cells), 0)
            q = [cells[v] + (section_a * section_b) * inc[v, x, at] for v in range(5)]
            own = [X["own"] * q[v] for v in range(5)]
            pair = [X["pair"] * f[v] for v in range(5)]
            plus = [a + b for a, b in zip(own, pair)]
            minus = [a - b for a, b in zip(own, pair)]
            if x == 0:
                totals = [plus, minus]
            else:
                totals[0] = [ROOT_F * a + b for a, b in zip(totals[0], plus)]
                totals[1] = [a + ROOT_F**x * b for a, b in zip(totals[1], minus)]
            for sign, j in ((1.0, x + 1), (-1.0, nx - x)):
                for k in range(3):
                    n = k + j
                    if n > 4:
                        continue
                    for v in range(5):
                        term = (sign * X["band_f"][n]) * f[v]
                        if n <= 3:
                            term = term + X["band_q"][n] * q[v]
                        so_far = ends[sign][k][v]
                        ends[sign][k][v] = term if so_far is None else so_far + term
            if x == 3:
                for k in range(3):
                    for v in range(5):
                        w_down[k, v, at] = ends[1.0][k][v]
        for v in range(5):
            base[0, v, at] = totals[0][v]
            base[1, v, at] = totals[1][v]
            for k in range(3):
                w_up[k, v, at] = ends[-1.0][k][v]
        return 0

    blocks.each(tile, rows // 8)


def fix_table(nz):
    weight = {1: 45.0, 2: -9.0, 3: 1.0}
    table = np.zeros((4 * nz, 2 * nz))
    for group in range(2):
        for place in range(nz // 8):
            into = group * nz + 8 * place
            came = 8 * place + 4 * group
            kept = (2 + group) * nz + 8 * place
            for j in range(3):
                for n, w in weight.items():
                    if j + n >= 3:
                        table[nz + came + j + n - 3, into + j] += w
                        table[kept + 3 + j + n - 3, into + j] -= w
                    if n > j:
                        table[came + 3 + j - n, into + 3 + j] -= w
                        table[kept + 3 + j - n, into + 3 + j] += w
    return table


def split(value):
    high = value.astype(jnp.bfloat16)
    return high, (value - high.astype(f32)).astype(jnp.bfloat16)


def around(at):
    return 45.0 * (at(1) - at(-1)) - 9.0 * (at(2) - at(-2)) + (at(3) - at(-3))


def along_lanes(h):
    v1 = roll(h, -1)
    v2 = roll(v1 - 9.0 * h, -2)
    both = 9.0 * v1 - h
    return 5.0 * both + v2 + roll(both + 5.0 * v2, 3)


def turn_of(x, nz):
    if isinstance(x, int):
        return (2 * nz - 3 - 8 * (x % 16)) % nz
    return lax.rem(2 * nz - 3 - 8 * lax.rem(x, 16), nz)


def end_kernel(
    base, w_up0, w_down0, g_rows, h_rows, y_halo, z_low, z_high, z_own, table,
    sums, own_sums, to_other, to_partner, fix, token, pad, dz_all,
):
    token[...] = jnp.zeros_like(token)
    ny, nz = base.shape[2:]
    nx = y_halo.shape[1] - 2
    lane = lanes((8, nz))
    edge_lane = (lane < 3) | (lane >= nz - 3)
    parts = [z_low[...], z_high[...], z_own[0], z_own[1]]
    halves = [split(p.reshape(5 * ny, nz)) for p in parts]
    fixed = sum(
        jnp.dot(jnp.concatenate([h[k] for h in halves], axis=1), table[...], preferred_element_type=f32)
        for k in range(2)
    )
    for group in range(2):
        fix[group] = fixed[:, group * nz : group * nz + nz].reshape(5, ny, nz)
    rows = [0, 1, 2, nx - 3, nx - 2, nx - 1, nx, nx + 1]
    for r, x in enumerate(rows):
        for v in range(5):
            pad[r, v, 0:8] = y_halo[v, x]
            pad[r, v, ny + 8 : ny + 16] = y_halo[v, x]

    def first(t, _):
        at = pl.ds(pl.multiple_of(8 * t, 8), 8)
        inside = pl.ds(pl.multiple_of(8 * t + 8, 8), 8)
        for r, x in enumerate(rows):
            for v in range(5):
                h = h_rows[r, v, at]
                pad[r, v, inside] = g_rows[r, v, at]
                moved = roll(fix[x // 16, v, at], turn_of(x, nz))
                dz_all[r, v, at] = along_lanes(h) + jnp.where(edge_lane, moved, 0.0)
        return 0

    lax.fori_loop(0, ny // 8, first, 0)
    scale = -time_step * section_b / 60.0

    odd = is_upper()

    def second(v, _):
        for t in range(ny // 8):
            at = slice(8 * t, 8 * t + 8)

            def cross(r, t=t, at=at):
                dy = around(lambda n: pad[r, v, 8 + 8 * t + n : 16 + 8 * t + n])
                return scale * (dy + dz_all[r, v, at])

            for k in range(2):
                sums[k, v, at] = own_sums[k, v, at] = base[k, v, at] + X["own"] * cross(6 + k)
            faces = []
            for begin, near in ((w_down0, (0, 1, 2)), (w_up0, (5, 4, 3))):
                q = [cross(r) for r in near]
                for k in range(3):
                    total = begin[k, v, at]
                    for j in range(1, 4 - k):
                        total = total + X["band_q"][k + j] * q[j - 1]
                    faces.append(total)
            for k in range(3):
                to_other[k, v, at] = jnp.where(odd, faces[3 + k], faces[k])
                to_partner[k, v, at] = jnp.where(odd, faces[k], faces[3 + k])
        return 0

    lax.fori_loop(0, 5, second, 0)


def part_kernel(
    begin, rho_hbm, mom_hbm, ene_hbm, inc_hbm, y_halo, fix, after,
    part, token,
    rho, mom, ene, inc, pad, sems,
):
    token[...] = jnp.zeros_like(token)
    nx, ny, nz = rho.shape
    lane = lanes((8, nz))
    edge_lane = (lane < 3) | (lane >= nz - 3)
    scale = -time_step / 60.0
    some = 4
    blocks = Blocks((rho_hbm, mom_hbm, ene_hbm, inc_hbm), (rho, mom, ene, inc), sems, (0, 1, 0, 1), some, begin)

    def one_row(x, _):
        turn = turn_of(begin + x, nz)
        group = (begin + x) // 16
        for v in range(5):
            pad[v, 0:8] = y_halo[v, begin + x]
            pad[v, ny + 8 : ny + 16] = y_halo[v, begin + x]
        for t in range(ny // 8):
            at = slice(8 * t, 8 * t + 8)
            cells = cells_at(rho, mom, ene, x, at)
            inverse, pressure = primitives(cells)
            g = flux(cells, inverse, pressure, 1)
            h = flux(cells, inverse, pressure, 2)
            for v in range(5):
                pad[v, 8 + 8 * t : 16 + 8 * t] = g[v]
                dz = along_lanes(h[v])
                dz = dz + jnp.where(edge_lane, roll(fix[group, v, at], turn), 0.0)
                part[v, x, at] = section_a * inc[v, x, at] + scale * dz
        for t in range(ny // 8):
            at = slice(8 * t, 8 * t + 8)
            for v in range(5):
                dy = around(lambda n, v=v, t=t: pad[v, 8 + 8 * t + n : 16 + 8 * t + n])
                part[v, x, at] = part[v, x, at] + scale * dy
        return 0

    blocks.each(one_row, some)


def line_kernel(rho_hbm, mom_hbm, ene_hbm, f_near, part0, part1, *rest):
    *sums, new_inc_hbm, local = rest[:-9]
    rho, mom, ene, new_inc, f_all, q_all, e_all, sems, out_sems = rest[-9:]
    nx, ny, nz = rho.shape
    rows = 16
    blocks = Blocks((rho_hbm, mom_hbm, ene_hbm), (rho, mom, ene), sems, (1, 2, 1), rows)

    def copy_of(k):
        at = pl.ds(pl.multiple_of(k * rows, rows), rows)
        return pltpu.make_async_copy(new_inc.at[:, :, at], new_inc_hbm.at[:, :, at], out_sems.at[k])

    def slab(k):
        blocks.wait(k)
        at = pl.ds(pl.multiple_of(k * rows, rows), rows)

        def fluxes_at(part, begin, x, _):
            cells = cells_at(rho, mom, ene, begin + x, at)
            for v, value in enumerate(flux(cells, *primitives(cells), 0)):
                f_all[v, begin + x] = value
                q_all[v, begin + x] = cells[v] + section_b * part[v, x, at]
            return 0

        cut = part0.shape[1]
        lax.fori_loop(0, cut, functools.partial(fluxes_at, part0, 0), 0)
        lax.fori_loop(0, nx - cut, functools.partial(fluxes_at, part1, cut), 0)
        lines_of = functools.partial(one_line, at, (part0, part1), f_near, sums, new_inc, local, f_all, q_all, e_all)
        lax.fori_loop(0, 5, lines_of, 0)

    write_out(slab, ny // rows, copy_of)


def one_line(at, parts, f_near, sums, new_inc, local, f_all, q_all, e_all, v, _):
    nx, cut = f_all.shape[1], parts[0].shape[1]
    f = [f_all[v, x] for x in range(nx)]
    q = [q_all[v, x] for x in range(nx)]
    near, other = f_near[v, at], sums[-1][2, v, at]
    low, high = jnp.where(is_upper(), near, other), jnp.where(is_upper(), other, near)
    from_low, from_high = incoming(ROOT_D**nx, sums, v, at)
    forward = ROOT_D * from_low
    for x in range(nx):
        e_all[x] = forward
        forward = ROOT_D * (f[x] + forward)
    backward = ROOT_D * from_high
    for x in reversed(range(nx)):
        e_all[x] = e_all[x] - backward
        backward = ROOT_D * (f[x] + backward)
    ahead = None
    for x in range(nx):
        before = low if x == 0 else f[x - 1]
        after = high if x == nx - 1 else f[x + 1]
        e = e_all[x]
        deriv = X["kappa"] * (after - before) + X["deriv"] * e
        new_inc[v, x, at] = (parts[0][v, x, at] if x < cut else parts[1][v, x - cut, at]) - time_step * deriv
        total = (1.0 - X["band_q"][0] - X["own"]) * q[x] - X["slow"] * e
        total = total - (section_b * time_step) * deriv
        for n in range(1, 4):
            near = [q[i] for i in (x - n, x + n) if 0 <= i < nx]
            total = total - X["band_q"][n] * (near[0] if len(near) == 1 else near[0] + near[1])
        for n in range(1, 5):
            if x + n < nx and x - n >= 0:
                total = total - X["band_f"][n] * (f[x + n] - f[x - n])
            elif x + n < nx:
                total = total - X["band_f"][n] * f[x + n]
            else:
                total = total + X["band_f"][n] * f[x - n]
        if x == 3:
            total = total + X["band_f"][4] * low
        if x == nx - 4:
            total = total - X["band_f"][4] * high
        if ahead is not None:
            total = total - ahead
        local[v, x, at] = total
        plus = X["own"] * q[x] + X["pair"] * f[x]
        ahead = ROOT_F * (plus if ahead is None else plus + ahead)
    behind = None
    for x in reversed(range(nx)):
        if behind is not None:
            local[v, x, at] = local[v, x, at] - behind
        minus = X["own"] * q[x] - X["pair"] * f[x]
        behind = ROOT_F * (minus if behind is None else minus + behind)
    return 0


def is_upper():
    return lax.axis_index("gx") % 2 == 1


def incoming(rate, sums, v, at):
    if len(sums) == 1:
        return sums[0][0, v, at], sums[0][1, v, at]
    beside, pair, opposite = sums
    closure = 1.0 / (1.0 - rate**4)
    low, high = (closure * (opposite[k, v, at] + rate**2 * pair[k, v, at]) for k in range(2))
    odd = is_upper()
    return (
        jnp.where(odd, beside[0, v, at] + rate * low, low),
        jnp.where(odd, high, beside[1, v, at] + rate * high),
    )


def mix_kernel(rate, own, came, after, *rest):
    *others, out, pair, beside, token = rest
    odd = is_upper()
    token[...] = jnp.zeros_like(token)
    for v in range(5):
        upper = jnp.where(odd, own[0, v] + rate * came[0, v], came[0, v] + rate * own[0, v])
        lower = jnp.where(odd, came[1, v] + rate * own[1, v], own[1, v] + rate * came[1, v])
        out[0, v] = pair[0, v] = upper
        out[1, v] = pair[1, v] = lower
        if others:
            taken, given, near = others
            near[v] = came[2, v]
            out[2, v] = came[3, v]
            for k in range(3):
                given[k, v] = taken[k, v]
    beside[0] = came[0]
    beside[1] = came[1]


def inner_kernel(local, *rest):
    *sums, out_hbm, rim, out, sems = rest
    nx = local.shape[1]

    def one(v):
        low, high = incoming(ROOT_F**nx, sums, v, slice(None))
        for x in range(nx):
            value = local[v, x] - (ROOT_F ** (x + 1)) * low - (ROOT_F ** (nx - x)) * high
            if 3 <= x < nx - 3:
                out[v, x] = value
            else:
                rim[x if x < 3 else x - nx + 6, v] = value

    inside = pl.ds(3, nx - 6)
    write_out(one, 5, lambda v: pltpu.make_async_copy(out.at[v, inside], out_hbm.at[v, inside], sems.at[v]))


def rim_kernel(before, rim, w_other, w_partner, out_hbm, out, sems):
    nx = out_hbm.shape[1]
    odd = is_upper()
    for k in range(3):
        for v in range(5):
            other, near = w_other[k, v], w_partner[k, v]
            out[0, v, k] = rim[k, v] - jnp.where(odd, near, other)
            out[1, v, 2 - k] = rim[5 - k, v] - jnp.where(odd, other, near)
    copies = [
        pltpu.make_async_copy(out.at[side], out_hbm.at[:, pl.ds(side * (nx - 3), 3)], sems.at[side]) for side in range(2)
    ]
    for copy in copies:
        copy.start()
    for copy in copies:
        copy.wait()


def shifted(value, axis, by):
    size = lax.axis_size(axis)
    return lax.ppermute(value, axis, [(i, (i + by) % size) for i in range(size)])


def ring_sums(own, rate):
    size = lax.axis_size("gx")
    gathered = lax.all_gather(own, "gx", axis=0)
    here = lax.axis_index("gx")
    member = jnp.arange(size, dtype=jnp.int32)
    table = jnp.asarray([rate**k / (1.0 - rate**size) for k in range(size)], f32)
    up = table[(here - 1 - member) % size]
    down = table[(member - here - 1) % size]
    shape = (size,) + (1,) * (own.ndim - 1)
    low = jnp.sum(up.reshape(shape) * gathered[:, 0], axis=0)
    high = jnp.sum(down.reshape(shape) * gathered[:, 1], axis=0)
    return jnp.stack([low, high])


def call(kernel, name, inputs, hbm, outputs, scratch, aliases=None):
    place = {True: pl.BlockSpec(memory_space=pltpu.HBM), False: pl.BlockSpec(memory_space=pltpu.VMEM)}
    shapes = [dims[1] if dims[0] == "hbm" else dims for dims in outputs]
    return pl.pallas_call(
        kernel,
        in_specs=[place[i < hbm] for i in range(len(inputs))],
        out_specs=[place[dims[0] == "hbm"] for dims in outputs],
        out_shape=[jax.ShapeDtypeStruct(dims, f32) for dims in shapes],
        scratch_shapes=scratch,
        input_output_aliases=aliases or {},
        compiler_params=pltpu.CompilerParams(vmem_limit_bytes=40 * 2**20),
        cost_estimate=pl.CostEstimate(flops=1000, bytes_accessed=1000, transcendentals=0),
        name=name,
    )(*[pltpu.with_memory_space_constraint(a, pltpu.HBM) if i < hbm else a for i, a in enumerate(inputs)])


def on_device(density, momentum, energy, increment):
    nx, ny, nz = density.shape
    members = lax.axis_size("gx")
    cells = nx * ny * nz
    state = (density, momentum, energy)
    face = (5, ny, nz)
    whole = (5, nx, ny, nz)

    def vmem(*dims):
        return pltpu.VMEM(dims, f32)

    def sems(*dims):
        return pltpu.SemaphoreType.DMA(dims)

    state_room = [vmem(nx, ny, nz), vmem(3, nx, ny, nz), vmem(nx, ny, nz)]

    to_partner, own_d, g_rows, h_rows, z_up, z_down, z_own, y_edge, begun = call(
        face_kernel,
        "faces",
        state,
        3,
        [(4, *face), (2, *face), (8, *face), (8, *face), face, face, (2, *face), (5, nx + 2, 8, nz), (8, nz)],
        state_room + [sems(3, ny // 16)],
    )
    z_low = shifted(z_up, "gz", 1)
    z_high = shifted(z_down, "gz", -1)
    y_halo = shifted(y_edge, "gy", 1)

    base, w_up0, w_down0 = call(
        base_kernel,
        "base",
        (*state, increment, begun),
        4,
        [(2, *face), (3, *face), (3, *face)],
        state_room + [vmem(*whole), sems(4, ny // 16)],
    )
    table = jnp.asarray(fix_table(nz), jnp.bfloat16)
    sums, own_sums, w_to_other, w_to_partner, fix, ended = call(
        end_kernel,
        "ends",
        (base, w_up0, w_down0, g_rows, h_rows, y_halo, z_low, z_high, z_own, table),
        0,
        [(2, *face), (2, *face), (3, *face), (3, *face), (2, *face), (8, nz)],
        [vmem(8, 5, ny + 16, nz), vmem(8, *face)],
    )
    rate_d, rate_f = ROOT_D**nx, ROOT_F**nx
    token = ended
    if members == 4:
        partner = [(i, i ^ 1) for i in range(members)]
        other = [(i, (i + 1 - 2 * (i % 2 == 0)) % members) for i in range(members)]
        mixed = [(2, *face), (2, *face), (8, nz)]
        d_came = lax.ppermute(to_partner, "gx", partner)
        f_came = lax.ppermute(sums, "gx", partner)
        w_partner = lax.ppermute(w_to_partner, "gx", partner)
        w_to_other, f_near, group, d_pair, d_beside, token = call(
            functools.partial(mix_kernel, rate_d),
            "mixd",
            (own_d, d_came, ended, w_to_other),
            0,
            [(3, *face), face, (3, *face)] + mixed,
            [],
        )
        w_other = lax.ppermute(w_to_other, "gx", other)
        far = (d_beside, d_pair, shifted(group, "gx", 2))
    else:
        odd = lax.axis_index("gx") % 2 == 1
        f_low = shifted(jnp.where(odd, to_partner[3], to_partner[2]), "gx", 1)
        f_high = shifted(jnp.where(odd, to_partner[2], to_partner[3]), "gx", -1)
        f_near, f_other = jnp.where(odd, f_low, f_high), jnp.where(odd, f_high, f_low)
        far = (jnp.concatenate([ring_sums(own_d, rate_d), f_other[None]]),)
        w_low = shifted(jnp.where(odd, w_to_other, w_to_partner), "gx", 1)
        w_high = shifted(jnp.where(odd, w_to_partner, w_to_other), "gx", -1)
        w_other, w_partner = jnp.where(odd, w_high, w_low), jnp.where(odd, w_low, w_high)
    cut = FIRST_ROWS
    parts = []
    for begin, rows in ((0, cut), (cut, nx - cut)):
        some_part, token = call(
            functools.partial(part_kernel, begin),
            "part%d" % begin,
            (*state, increment, y_halo, fix, token),
            4,
            [(5, rows, ny, nz), (8, nz)],
            [vmem(rows, ny, nz), vmem(3, rows, ny, nz), vmem(rows, ny, nz), vmem(5, rows, ny, nz)]
            + [vmem(5, ny + 16, nz), sems(4, rows // 4)],
        )
        parts.append(some_part)
        if begin == 0 and members == 4:
            group, f_pair, f_beside, token = call(
                functools.partial(mix_kernel, rate_f), "mixf", (own_sums, f_came, token), 0, [(2, *face)] + mixed, []
            )
            from_others = (f_beside, f_pair, shifted(group, "gx", 2))
    if members != 4:
        from_others = (ring_sums(own_sums, rate_f),)
    new_increment, local = call(
        line_kernel,
        "lines",
        (*state, f_near, *parts, *far),
        3,
        [("hbm", whole), whole],
        state_room
        + [vmem(*whole), vmem(5, nx, 16, nz), vmem(5, nx, 16, nz), vmem(nx, 16, nz)]
        + [sems(3, ny // 16), sems(ny // 16)],
    )
    inner, rim = call(
        inner_kernel,
        "inner",
        (local, *from_others),
        0,
        [("hbm", whole), (6, *face)],
        [vmem(*whole), sems(5)],
    )
    (new_state,) = call(
        rim_kernel,
        "rim",
        (inner, rim, w_other, w_partner),
        1,
        [("hbm", whole)],
        [vmem(2, 5, 3, ny, nz), sems(2)],
        {0: 0},
    )
    return (new_state, new_increment)


def solution(mesh):
    in_specs = (
        P("gx", "gy", "gz"),
        P(None, "gx", "gy", "gz"),
        P("gx", "gy", "gz"),
        P(None, "gx", "gy", "gz"),
    )
    out_specs = (P(None, "gx", "gy", "gz"), P(None, "gx", "gy", "gz"))
    return jax.shard_map(
        on_device, mesh=mesh, in_specs=in_specs, out_specs=out_specs, check_vma=False
    )
```

```python
import functools
import math

import jax
import jax.numpy as jnp
import numpy as np
from jax import lax
from jax.experimental import pallas as pl
from jax.experimental.pallas import tpu as pltpu
from jax.sharding import PartitionSpec as P

deriv_alpha = 1.0 / 3.0
filter_alpha = 0.4999
gas_gamma = 1.4
time_step = 0.2
section_a = -5.0 / 9.0
section_b = 15.0 / 16.0
explicit_weights = (0.75, -0.15, 1.0 / 60.0)
f32 = jnp.float32
CUTS = (0, 4, 12)


def root_of(coupling):
    return (-1.0 + math.sqrt(1.0 - 4.0 * coupling * coupling)) / (2.0 * coupling)


def laurent(poly, times_s):
    size = len(poly) + 1
    total = np.zeros(2 * size + 1)
    for power, value in enumerate(poly):
        term = np.array([1.0])
        for _ in range(power):
            term = np.convolve(term, [1.0, 0.0, 1.0])
        if times_s:
            term = np.convolve(term, [-1.0, 0.0, 1.0])
        half = len(term) // 2
        total[size - half : size + half + 1] += value * term
    return [float(v) for v in total[size:]]


def x_constants():
    ad, af = deriv_alpha, filter_alpha
    kappa = (1.0 / 36.0) / ad
    beta = 7.0 / 9.0 - kappa
    poly = np.polynomial.polynomial
    p_of_c = (1.0 - 2.0 * af) / 256.0 * poly.polypow([2.0, -1.0], 4)
    q_of_c, rest = poly.polydiv(p_of_c, [1.0, af])
    rho = float(rest[0])
    both = poly.polymul([1.0, af], [1.0, ad])
    q2_of_c, _ = poly.polydiv(p_of_c, both)
    mu_f = float(poly.polyval(-1.0 / af, p_of_c)) / (1.0 - ad / af)
    mu_d = float(poly.polyval(-1.0 / ad, p_of_c)) / (1.0 - af / ad)
    b_of_c = poly.polyadd(kappa * q_of_c, beta * q2_of_c)
    g = 1.0 / math.sqrt(1.0 - 4.0 * af * af)
    sigma = -section_b * time_step
    return dict(
        kappa=kappa,
        deriv=beta / ad,
        band_q=laurent(q_of_c, False)[:4],
        band_f=[sigma * v for v in laurent(b_of_c, True)[:5]],
        own=rho * g,
        pair=sigma * (kappa * rho + beta * mu_f) / af,
        slow=sigma * beta * mu_d / ad,
    )


X = x_constants()
ROOT_D = root_of(deriv_alpha)
ROOT_F = root_of(filter_alpha)


def primitives(cells):
    density, m0, m1, m2, energy = cells
    inverse = 1.0 / density
    squared = m0 * m0 + m1 * m1 + m2 * m2
    pressure = (gas_gamma - 1.0) * (energy - 0.5 * squared * inverse)
    return inverse, pressure


def flux(cells, inverse, pressure, axis_k):
    momentum = cells[1:4]
    velocity = momentum[axis_k] * inverse
    parts = [
        momentum[axis_k],
        momentum[0] * velocity,
        momentum[1] * velocity,
        momentum[2] * velocity,
        (cells[4] + pressure) * velocity,
    ]
    parts[axis_k + 1] = parts[axis_k + 1] + pressure
    return parts


def lanes(shape):
    return lax.broadcasted_iota(jnp.int32, shape, len(shape) - 1)


def roll(value, amount):
    size = value.shape[-1]
    if isinstance(amount, int):
        amount = amount % size
        if amount == 0:
            return value
    return pltpu.roll(value, amount, value.ndim - 1)


class Blocks:
    def __init__(self, sources, targets, sems, dims, size, begin=0):
        self.parts = list(zip(sources, targets, dims, strict=True))
        self.sems, self.size, self.begin = sems, size, begin
        self.count = targets[0].shape[dims[0]] // size

        def start(k, _):
            for copy in self.piece(k):
                copy.start()
            return 0

        lax.fori_loop(0, self.count, start, 0)

    def piece(self, k):
        copies = []
        for n, (source, target, dim) in enumerate(self.parts):
            lead = (slice(None),) * dim
            first = pl.multiple_of(k * self.size, self.size)
            there = source.at[(*lead, pl.ds(self.begin + first, self.size))]
            here = target.at[(*lead, pl.ds(first, self.size))]
            copies.append(pltpu.make_async_copy(there, here, self.sems.at[n, k]))
        return copies

    def wait(self, k):
        for copy in self.piece(k):
            copy.wait()

    def each(self, body, steps):
        def one(k, _):
            self.wait(k)
            lax.fori_loop(k * steps, (k + 1) * steps, body, 0)
            return 0

        lax.fori_loop(0, self.count, one, 0)


def write_out(kernel_part, pieces, copy_of):
    def one(k, _):
        kernel_part(k)
        copy_of(k).start()
        return 0

    def wait(k, _):
        copy_of(k).wait()
        return 0

    lax.fori_loop(0, pieces, one, 0)
    lax.fori_loop(0, pieces, wait, 0)


def cells_at(rho, mom, ene, x, at):
    return [rho[x, at], mom[0, x, at], mom[1, x, at], mom[2, x, at], ene[x, at]]


def face_kernel(
    rho_hbm, mom_hbm, ene_hbm,
    d_out, f_out, own, g_rows, h_rows, z_up, z_down, z_own, y_edge, token,
    rho, mom, ene, sems,
):
    nx, ny, nz = rho.shape
    lane = lanes((8, nz))
    slot = lane // 8
    first_half = lane % 8 < 4
    row = lax.broadcasted_iota(jnp.int32, (8, nz), 0)
    stored = {x: r for r, x in enumerate((0, 1, 2, nx - 3, nx - 2, nx - 1))}
    rows = 16
    blocks = Blocks((rho_hbm, mom_hbm, ene_hbm), (rho, mom, ene), sems, (1, 2, 1), rows)
    token[...] = jnp.zeros_like(token)
    odd = is_upper()

    def tile(t, _):
        at = pl.ds(pl.multiple_of(8 * t, 8), 8)
        keep = (row < 4) & (t > 0)
        packed = [[None] * 5, [None] * 5]
        totals = lower = upper = None
        for x in range(nx):
            cells = cells_at(rho, mom, ene, x, at)
            inverse, pressure = primitives(cells)
            f = flux(cells, inverse, pressure, 0)
            g = flux(cells, inverse, pressure, 1)
            h = flux(cells, inverse, pressure, 2)
            group, place = x // 16, x % 16
            for v in range(5):
                y_edge[v, x] = jnp.where(keep, y_edge[v, x], g[v])
                moved = roll(cells[v], 8 * place + 3)
                if place:
                    moved = jnp.where(slot == place, moved, packed[group][v])
                packed[group][v] = moved
                if x in stored:
                    g_rows[stored[x], v, at] = g[v]
                    h_rows[stored[x], v, at] = h[v]
                if x == 0:
                    f_out[0, v, at] = f[v]
                if x == nx - 1:
                    first = f_out[0, v, at]
                    f_out[0, v, at] = jnp.where(odd, first, f[v])
                    f_out[1, v, at] = jnp.where(odd, f[v], first)
            if x == 0:
                totals, lower, upper = [g, h, g, h], f, f
            else:
                lower = [ROOT_D * a + b for a, b in zip(lower, f)]
                upper = [a + ROOT_D**x * b for a, b in zip(upper, f)]
                factor = ROOT_F**x
                totals = [
                    [ROOT_F * a + b if k < 2 else a + factor * b for a, b in zip(total, term)]
                    for k, (total, term) in enumerate(zip(totals, (g, h, g, h)))
                ]
        h = [flux(packed[group], *primitives(packed[group]), 2) for group in range(2)]
        for v in range(5):
            d_out[0, v, at] = own[0, v, at] = lower[v]
            d_out[1, v, at] = own[1, v, at] = upper[v]
            for k in range(2):
                g_rows[6 + k, v, at] = totals[2 * k][v]
                h_rows[6 + k, v, at] = totals[2 * k + 1][v]
                y_edge[v, nx + k] = jnp.where(keep, y_edge[v, nx + k], totals[2 * k][v])
                group, place = (nx + k) // 16, (nx + k) % 16
                moved = roll(totals[2 * k + 1][v], 8 * place + 3)
                h[group][v] = jnp.where(slot == place, moved, h[group][v])
            for group in range(2):
                z_own[group, v, at] = h[group][v]
            z_up[v, at] = jnp.where(first_half, h[0][v], roll(h[1][v], 4))
            z_down[v, at] = jnp.where(first_half, roll(h[0][v], -3), roll(h[1][v], 1))
        return 0

    blocks.each(tile, rows // 8)


def base_kernel(rho_hbm, mom_hbm, ene_hbm, inc_hbm, after, base, w_up, w_down, token, rho, mom, ene, inc, sems):
    token[...] = jnp.zeros_like(token)
    nx, ny, nz = rho.shape
    rows = 16
    blocks = Blocks((rho_hbm, mom_hbm, ene_hbm, inc_hbm), (rho, mom, ene, inc), sems, (1, 2, 1, 2), rows)

    def tile(t, _):
        at = pl.ds(pl.multiple_of(8 * t, 8), 8)
        totals = None
        ends = {1.0: [[None] * 5 for _ in range(3)], -1.0: [[None] * 5 for _ in range(3)]}
        for x in range(nx):
            cells = cells_at(rho, mom, ene, x, at)
            f = flux(cells, *primitives(cells), 0)
            q = [cells[v] + (section_a * section_b) * inc[v, x, at] for v in range(5)]
            own = [X["own"] * q[v] for v in range(5)]
            pair = [X["pair"] * f[v] for v in range(5)]
            plus = [a + b for a, b in zip(own, pair)]
            minus = [a - b for a, b in zip(own, pair)]
            if x == 0:
                totals = [plus, minus]
            else:
                totals[0] = [ROOT_F * a + b for a, b in zip(totals[0], plus)]
                totals[1] = [a + ROOT_F**x * b for a, b in zip(totals[1], minus)]
            for sign, j in ((1.0, x + 1), (-1.0, nx - x)):
                for k in range(3):
                    n = k + j
                    if n > 4:
                        continue
                    for v in range(5):
                        term = (sign * X["band_f"][n]) * f[v]
                        if n <= 3:
                            term = term + X["band_q"][n] * q[v]
                        so_far = ends[sign][k][v]
                        ends[sign][k][v] = term if so_far is None else so_far + term
            if x == 3:
                for k in range(3):
                    for v in range(5):
                        w_down[k, v, at] = ends[1.0][k][v]
        for v in range(5):
            base[0, v, at] = totals[0][v]
            base[1, v, at] = totals[1][v]
            for k in range(3):
                w_up[k, v, at] = ends[-1.0][k][v]
        return 0

    blocks.each(tile, rows // 8)


def fix_table(nz):
    weight = {1: 45.0, 2: -9.0, 3: 1.0}
    table = np.zeros((4 * nz, 2 * nz))
    for group in range(2):
        for place in range(nz // 8):
            into = group * nz + 8 * place
            came = 8 * place + 4 * group
            kept = (2 + group) * nz + 8 * place
            for j in range(3):
                for n, w in weight.items():
                    if j + n >= 3:
                        table[nz + came + j + n - 3, into + j] += w
                        table[kept + 3 + j + n - 3, into + j] -= w
                    if n > j:
                        table[came + 3 + j - n, into + 3 + j] -= w
                        table[kept + 3 + j - n, into + 3 + j] += w
    return table


def split(value):
    high = value.astype(jnp.bfloat16)
    return high, (value - high.astype(f32)).astype(jnp.bfloat16)


def around(at):
    return 45.0 * (at(1) - at(-1)) - 9.0 * (at(2) - at(-2)) + (at(3) - at(-3))


def along_lanes(h):
    v1 = roll(h, -1)
    v2 = roll(v1 - 9.0 * h, -2)
    both = 9.0 * v1 - h
    return 5.0 * both + v2 + roll(both + 5.0 * v2, 3)


def turn_of(x, nz):
    if isinstance(x, int):
        return (2 * nz - 3 - 8 * (x % 16)) % nz
    return lax.rem(2 * nz - 3 - 8 * lax.rem(x, 16), nz)


def end_rows(nx):
    return [0, 1, 2, nx - 3, nx - 2, nx - 1, nx, nx + 1]


def add_cross(cross, sums, w_up, w_down):
    scale = -time_step * section_b / 60.0
    for k in range(2):
        sums[k] = sums[k] + (scale * X["own"]) * cross[6 + k]
    for w, near in ((w_down, (0, 1, 2)), (w_up, (5, 4, 3))):
        for k in range(3):
            for j in range(1, 4 - k):
                w[k] = w[k] + (scale * X["band_q"][k + j]) * cross[near[j - 1]]


def early_kernel(base, w_up0, w_down0, g_rows, h_rows, y_halo, after, sums, w_up, w_down, pad):
    ny, nz = base.shape[2:]
    nx = y_halo.shape[1] - 2
    for r, x in enumerate(end_rows(nx)):
        for v in range(5):
            pad[r, v, 0:8] = y_halo[v, x]
            pad[r, v, ny + 8 : ny + 16] = y_halo[v, x]
            pad[r, v, 8 : ny + 8] = g_rows[r, v]

    def one(v, _):
        for t in range(ny // 8):
            at = slice(8 * t, 8 * t + 8)
            cross = []
            for r in range(8):
                dy = around(lambda n, r=r, t=t: pad[r, v, 8 + 8 * t + n : 16 + 8 * t + n])
                cross.append(dy + along_lanes(h_rows[r, v, at]))
            parts = [[ref[k, v, at] for k in range(ref.shape[0])] for ref in (base, w_up0, w_down0)]
            add_cross(cross, *parts)
            for ref, part in zip((sums, w_up, w_down), parts, strict=True):
                for k, value in enumerate(part):
                    ref[k, v, at] = value
        return 0

    lax.fori_loop(0, 5, one, 0)


def end_kernel(
    nx, sums0, w_up0, w_down0, z_low, z_high, z_own, table,
    sums, own_sums, to_other, to_partner, fix, token,
):
    token[...] = jnp.zeros_like(token)
    ny, nz = sums0.shape[2:]
    lane = lanes((8, nz))
    edge_lane = (lane < 3) | (lane >= nz - 3)
    parts = [z_low[...], z_high[...], z_own[0], z_own[1]]
    halves = [split(p.reshape(5 * ny, nz)) for p in parts]
    fixed = sum(
        jnp.dot(jnp.concatenate([h[k] for h in halves], axis=1), table[...], preferred_element_type=f32)
        for k in range(2)
    )
    for group in range(2):
        fix[group] = fixed[:, group * nz : group * nz + nz].reshape(5, ny, nz)
    odd = is_upper()

    def one(v, _):
        for t in range(ny // 8):
            at = slice(8 * t, 8 * t + 8)
            cross = [
                jnp.where(edge_lane, roll(fix[x // 16, v, at], turn_of(x, nz)), 0.0) for x in end_rows(nx)
            ]
            parts = [[ref[k, v, at] for k in range(ref.shape[0])] for ref in (sums0, w_up0, w_down0)]
            add_cross(cross, *parts)
            for k in range(2):
                sums[k, v, at] = own_sums[k, v, at] = parts[0][k]
            for k in range(3):
                to_other[k, v, at] = jnp.where(odd, parts[1][k], parts[2][k])
                to_partner[k, v, at] = jnp.where(odd, parts[2][k], parts[1][k])
        return 0

    lax.fori_loop(0, 5, one, 0)


def part_kernel(
    begin, rho_hbm, mom_hbm, ene_hbm, inc_hbm, y_halo, fix, after,
    part, token,
    rho, mom, ene, inc, pad, sems,
):
    token[...] = jnp.zeros_like(token)
    nx, ny, nz = rho.shape
    lane = lanes((8, nz))
    edge_lane = (lane < 3) | (lane >= nz - 3)
    scale = -time_step / 60.0
    some = 4
    blocks = Blocks((rho_hbm, mom_hbm, ene_hbm, inc_hbm), (rho, mom, ene, inc), sems, (0, 1, 0, 1), some, begin)

    def one_row(x, _):
        turn = turn_of(begin + x, nz)
        group = (begin + x) // 16
        for v in range(5):
            pad[v, 0:8] = y_halo[v, begin + x]
            pad[v, ny + 8 : ny + 16] = y_halo[v, begin + x]
        for t in range(ny // 8):
            at = slice(8 * t, 8 * t + 8)
            cells = cells_at(rho, mom, ene, x, at)
            inverse, pressure = primitives(cells)
            g = flux(cells, inverse, pressure, 1)
            h = flux(cells, inverse, pressure, 2)
            for v in range(5):
                pad[v, 8 + 8 * t : 16 + 8 * t] = g[v]
                dz = along_lanes(h[v])
                dz = dz + jnp.where(edge_lane, roll(fix[group, v, at], turn), 0.0)
                part[v, x, at] = section_a * inc[v, x, at] + scale * dz
        for t in range(ny // 8):
            at = slice(8 * t, 8 * t + 8)
            for v in range(5):
                dy = around(lambda n, v=v, t=t: pad[v, 8 + 8 * t + n : 16 + 8 * t + n])
                part[v, x, at] = part[v, x, at] + scale * dy
        return 0

    blocks.each(one_row, some)


def line_kernel(count, rho_hbm, mom_hbm, ene_hbm, f_near, *rest):
    parts, rest = rest[:count], rest[count:]
    *sums, new_inc_hbm, local, edges = rest[:-9]
    rho, mom, ene, new_inc, f_all, q_all, e_all, sems, out_sems = rest[-9:]
    nx, ny, nz = rho.shape
    rows = 16
    blocks = Blocks((rho_hbm, mom_hbm, ene_hbm), (rho, mom, ene), sems, (1, 2, 1), rows)

    def copy_of(k):
        at = pl.ds(pl.multiple_of(k * rows, rows), rows)
        return pltpu.make_async_copy(new_inc.at[:, :, at], new_inc_hbm.at[:, :, at], out_sems.at[k])

    def slab(k):
        blocks.wait(k)
        at = pl.ds(pl.multiple_of(k * rows, rows), rows)

        def fluxes_at(part, begin, x, _):
            cells = cells_at(rho, mom, ene, begin + x, at)
            for v, value in enumerate(flux(cells, *primitives(cells), 0)):
                f_all[v, begin + x] = value
                q_all[v, begin + x] = cells[v] + section_b * part[v, x, at]
            return 0

        begin = 0
        for part in parts:
            lax.fori_loop(0, part.shape[1], functools.partial(fluxes_at, part, begin), 0)
            begin += part.shape[1]
        lines_of = functools.partial(one_line, at, parts, f_near, sums, new_inc, local, edges, f_all, q_all, e_all)
        lax.fori_loop(0, 5, lines_of, 0)

    write_out(slab, ny // rows, copy_of)


def one_line(at, parts, f_near, sums, new_inc, local, edges, f_all, q_all, e_all, v, _):
    nx = f_all.shape[1]
    part_at = [(part, i) for part in parts for i in range(part.shape[1])]
    f = [f_all[v, x] for x in range(nx)]
    q = [q_all[v, x] for x in range(nx)]
    near = f_near[v, at]
    low, high = jnp.where(is_upper(), near, 0.0), jnp.where(is_upper(), 0.0, near)
    from_low, from_high = incoming(ROOT_D**nx, sums, v, at)
    forward = ROOT_D * from_low
    for x in range(nx):
        e_all[x] = forward
        forward = ROOT_D * (f[x] + forward)
    backward = ROOT_D * from_high
    for x in reversed(range(nx)):
        e_all[x] = e_all[x] - backward
        backward = ROOT_D * (f[x] + backward)
    ahead = None
    for x in range(nx):
        before = low if x == 0 else f[x - 1]
        after = high if x == nx - 1 else f[x + 1]
        e = e_all[x]
        deriv = X["kappa"] * (after - before) + X["deriv"] * e
        value = part_at[x][0][v, part_at[x][1], at] - time_step * deriv
        new_inc[v, x, at] = value
        if x in (0, nx - 1):
            edges[x // (nx - 1), v, at] = value
        total = (1.0 - X["band_q"][0] - X["own"]) * q[x] - X["slow"] * e
        total = total - (section_b * time_step) * deriv
        for n in range(1, 4):
            near = [q[i] for i in (x - n, x + n) if 0 <= i < nx]
            total = total - X["band_q"][n] * (near[0] if len(near) == 1 else near[0] + near[1])
        for n in range(1, 5):
            if x + n < nx and x - n >= 0:
                total = total - X["band_f"][n] * (f[x + n] - f[x - n])
            elif x + n < nx:
                total = total - X["band_f"][n] * f[x + n]
            else:
                total = total + X["band_f"][n] * f[x - n]
        if x == 3:
            total = total + X["band_f"][4] * low
        if x == nx - 4:
            total = total - X["band_f"][4] * high
        if ahead is not None:
            total = total - ahead
        local[v, x, at] = total
        plus = X["own"] * q[x] + X["pair"] * f[x]
        ahead = ROOT_F * (plus if ahead is None else plus + ahead)
    behind = None
    for x in reversed(range(nx)):
        if behind is not None:
            local[v, x, at] = local[v, x, at] - behind
        minus = X["own"] * q[x] - X["pair"] * f[x]
        behind = ROOT_F * (minus if behind is None else minus + behind)
    return 0


def is_upper():
    return lax.axis_index("gx") % 2 == 1


def incoming(rate, sums, v, at):
    if len(sums) == 1:
        return sums[0][0, v, at], sums[0][1, v, at]
    beside, pair, opposite = sums
    closure = 1.0 / (1.0 - rate**4)
    low, high = (closure * (opposite[k, v, at] + rate**2 * pair[k, v, at]) for k in range(2))
    odd = is_upper()
    return (
        jnp.where(odd, beside[0, v, at] + rate * low, low),
        jnp.where(odd, high, beside[1, v, at] + rate * high),
    )


def mix_kernel(rate, own, came, after, *rest):
    *others, out, pair, beside, token = rest
    odd = is_upper()
    token[...] = jnp.zeros_like(token)
    for v in range(5):
        upper = jnp.where(odd, own[0, v] + rate * came[0, v], came[0, v] + rate * own[0, v])
        lower = jnp.where(odd, came[1, v] + rate * own[1, v], own[1, v] + rate * came[1, v])
        out[0, v] = pair[0, v] = upper
        out[1, v] = pair[1, v] = lower
    beside[...] = came[...]
    if others:
        halos, f_came, d_came, halos_out, f_out, d_out = others
        halos_out[...] = halos[...]
        f_out[...] = f_came[...]
        d_out[...] = d_came[...]


def pass_kernel(came, after, near, onward, token):
    token[...] = jnp.zeros_like(token)
    near[...] = came[0]
    onward[...] = came[1]


def inner_kernel(local, w_partner, *rest):
    *sums, out_hbm, rim, out, sems = rest
    nx = local.shape[1]
    odd = is_upper()

    def one(v):
        low, high = incoming(ROOT_F**nx, sums, v, slice(None))
        for x in range(nx):
            value = local[v, x] - (ROOT_F ** (x + 1)) * low - (ROOT_F ** (nx - x)) * high
            if x < 3:
                value = value - jnp.where(odd, w_partner[x, v], 0.0)
            if x >= nx - 3:
                value = value - jnp.where(odd, 0.0, w_partner[nx - 1 - x, v])
            if 4 <= x < nx - 4:
                out[v, x] = value
            else:
                rim[x if x < 4 else x - nx + 8, v] = value

    inside = pl.ds(4, nx - 8)
    write_out(one, 5, lambda v: pltpu.make_async_copy(out.at[v, inside], out_hbm.at[v, inside], sems.at[v]))


def rim_kernel(before, inc_before, rim, edges, f_other, w_other, out_hbm, inc_hbm, out, inc, sems):
    nx = out_hbm.shape[1]
    odd = is_upper()
    step = time_step * X["kappa"]
    for v in range(5):
        for side in range(2):
            others = odd if side else jnp.logical_not(odd)
            sign = -1.0 if side else 1.0
            far = sign * jnp.where(others, f_other[v], 0.0)
            for k in range(4):
                value = rim[7 - k if side else k, v]
                if k < 3:
                    value = value - jnp.where(others, w_other[k, v], 0.0)
                if k == 0:
                    value = value + (section_b * step) * far
                if k == 3:
                    value = value + X["band_f"][4] * far
                out[side, v, 3 - k if side else k] = value
            inc[side, v, 0] = edges[side, v] + step * far
    copies = []
    for side in range(2):
        rows, row = pl.ds(side * (nx - 4), 4), pl.ds(side * (nx - 1), 1)
        copies.append(pltpu.make_async_copy(out.at[side], out_hbm.at[:, rows], sems.at[0, side]))
        copies.append(pltpu.make_async_copy(inc.at[side], inc_hbm.at[:, row], sems.at[1, side]))
    for copy in copies:
        copy.start()
    for copy in copies:
        copy.wait()


def shifted(value, axis, by):
    size = lax.axis_size(axis)
    return lax.ppermute(value, axis, [(i, (i + by) % size) for i in range(size)])


def ring_sums(own, rate):
    size = lax.axis_size("gx")
    gathered = lax.all_gather(own, "gx", axis=0)
    here = lax.axis_index("gx")
    member = jnp.arange(size, dtype=jnp.int32)
    table = jnp.asarray([rate**k / (1.0 - rate**size) for k in range(size)], f32)
    up = table[(here - 1 - member) % size]
    down = table[(member - here - 1) % size]
    shape = (size,) + (1,) * (own.ndim - 1)
    low = jnp.sum(up.reshape(shape) * gathered[:, 0], axis=0)
    high = jnp.sum(down.reshape(shape) * gathered[:, 1], axis=0)
    return jnp.stack([low, high])


def call(kernel, name, inputs, hbm, outputs, scratch, aliases=None):
    place = {True: pl.BlockSpec(memory_space=pltpu.HBM), False: pl.BlockSpec(memory_space=pltpu.VMEM)}
    shapes = [dims[1] if dims[0] == "hbm" else dims for dims in outputs]
    return pl.pallas_call(
        kernel,
        in_specs=[place[i < hbm] for i in range(len(inputs))],
        out_specs=[place[dims[0] == "hbm"] for dims in outputs],
        out_shape=[jax.ShapeDtypeStruct(dims, f32) for dims in shapes],
        scratch_shapes=scratch,
        input_output_aliases=aliases or {},
        compiler_params=pltpu.CompilerParams(vmem_limit_bytes=40 * 2**20),
        cost_estimate=pl.CostEstimate(flops=1000, bytes_accessed=1000, transcendentals=0),
        name=name,
    )(*[pltpu.with_memory_space_constraint(a, pltpu.HBM) if i < hbm else a for i, a in enumerate(inputs)])


def on_device(density, momentum, energy, increment):
    nx, ny, nz = density.shape
    members = lax.axis_size("gx")
    cells = nx * ny * nz
    state = (density, momentum, energy)
    face = (5, ny, nz)
    whole = (5, nx, ny, nz)

    def vmem(*dims):
        return pltpu.VMEM(dims, f32)

    def sems(*dims):
        return pltpu.SemaphoreType.DMA(dims)

    state_room = [vmem(nx, ny, nz), vmem(3, nx, ny, nz), vmem(nx, ny, nz)]

    d_out, f_out, own_d, g_rows, h_rows, z_up, z_down, z_own, y_edge, begun = call(
        face_kernel,
        "faces",
        state,
        3,
        [(2, *face), (2, *face), (2, *face), (8, *face), (8, *face), face, face, (2, *face), (5, nx + 2, 8, nz), (8, nz)],
        state_room + [sems(3, ny // 16)],
    )
    z_low = shifted(z_up, "gz", 1)
    z_high = shifted(z_down, "gz", -1)
    y_halo = shifted(y_edge, "gy", 1)

    base, w_up0, w_down0, based = call(
        base_kernel,
        "base",
        (*state, increment, begun),
        4,
        [(2, *face), (3, *face), (3, *face), (8, nz)],
        state_room + [vmem(*whole), sems(4, ny // 16)],
    )
    table = jnp.asarray(fix_table(nz), jnp.bfloat16)
    rate_d, rate_f = ROOT_D**nx, ROOT_F**nx
    token = based
    partner = [(i, i ^ 1) for i in range(members)]
    other = [(i, (i + 1 - 2 * (i % 2 == 0)) % members) for i in range(members)]
    mixed = [(2, *face), (2, *face), (8, nz)]
    if members == 4:
        d_came = lax.ppermute(d_out, "gx", partner)
        f_came = lax.ppermute(f_out, "gx", partner)
        group, d_pair, d_beside, token = call(
            functools.partial(mix_kernel, rate_d), "mixd", (own_d, d_came, based), 0, [(2, *face)] + mixed, []
        )
        d_opposite = shifted(group, "gx", 2)
    sums0, w_up1, w_down1 = call(
        early_kernel,
        "early",
        (base, w_up0, w_down0, g_rows, h_rows, y_halo, token),
        0,
        [(2, *face), (3, *face), (3, *face)],
        [vmem(8, 5, ny + 16, nz)],
    )
    sums, own_sums, w_to_other, w_to_partner, fix, ended = call(
        functools.partial(end_kernel, nx),
        "ends",
        (sums0, w_up1, w_down1, z_low, z_high, z_own, table),
        0,
        [(2, *face), (2, *face), (3, *face), (3, *face), (2, *face), (8, nz)],
        [],
    )
    token = ended
    if members == 4:
        sums_came = lax.ppermute(sums, "gx", partner)
        w_partner = lax.ppermute(w_to_partner, "gx", partner)
    else:
        odd = lax.axis_index("gx") % 2 == 1
        f_low = shifted(jnp.where(odd, f_out[1], f_out[0]), "gx", 1)
        f_high = shifted(jnp.where(odd, f_out[0], f_out[1]), "gx", -1)
        f_near, f_other = jnp.where(odd, f_low, f_high), jnp.where(odd, f_high, f_low)
        far = (ring_sums(own_d, rate_d),)
        w_low = shifted(jnp.where(odd, w_to_other, w_to_partner), "gx", 1)
        w_high = shifted(jnp.where(odd, w_to_partner, w_to_other), "gx", -1)
        w_other, w_partner = jnp.where(odd, w_high, w_low), jnp.where(odd, w_low, w_high)
    parts = []
    for begin, end in zip(CUTS, CUTS[1:] + (nx,), strict=True):
        rows = end - begin
        some_part, token = call(
            functools.partial(part_kernel, begin),
            "part%d" % begin,
            (*state, increment, y_halo, fix, token),
            4,
            [(5, rows, ny, nz), (8, nz)],
            [vmem(rows, ny, nz), vmem(3, rows, ny, nz), vmem(rows, ny, nz), vmem(5, rows, ny, nz)]
            + [vmem(5, ny + 16, nz), sems(4, rows // 4)],
        )
        parts.append(some_part)
        if len(parts) == 1 and members == 4:
            f_near, onward, token = call(pass_kernel, "pass", (f_came, token), 0, [face, face, (8, nz)], [])
            f_passed = shifted(onward, "gx", 2)
        if len(parts) == 2 and members == 4:
            w_to_other, f_other, d_opposite, group, f_pair, f_beside, token = call(
                functools.partial(mix_kernel, rate_f),
                "mixf",
                (own_sums, sums_came, token, w_to_other, f_passed, d_opposite),
                0,
                [(3, *face), face, (2, *face), (2, *face)] + mixed,
                [],
            )
            far = (d_beside, d_pair, d_opposite)
            w_other = lax.ppermute(w_to_other, "gx", other)
            from_others = (f_beside, f_pair, shifted(group, "gx", 2))
    if members != 4:
        from_others = (ring_sums(own_sums, rate_f),)
    new_inc, local, edges = call(
        functools.partial(line_kernel, len(parts)),
        "lines",
        (*state, f_near, *parts, *far),
        3,
        [("hbm", whole), whole, (2, *face)],
        state_room
        + [vmem(*whole), vmem(5, nx, 16, nz), vmem(5, nx, 16, nz), vmem(nx, 16, nz)]
        + [sems(3, ny // 16), sems(ny // 16)],
    )
    inner, rim = call(
        inner_kernel,
        "inner",
        (local, w_partner, *from_others),
        0,
        [("hbm", whole), (8, *face)],
        [vmem(*whole), sems(5)],
    )
    new_state, new_increment = call(
        rim_kernel,
        "rim",
        (inner, new_inc, rim, edges, f_other, w_other),
        2,
        [("hbm", whole), ("hbm", whole)],
        [vmem(2, 5, 4, ny, nz), vmem(2, 5, 1, ny, nz), sems(2, 2)],
        {0: 0, 1: 1},
    )
    return (new_state, new_increment)


def solution(mesh):
    in_specs = (
        P("gx", "gy", "gz"),
        P(None, "gx", "gy", "gz"),
        P("gx", "gy", "gz"),
        P(None, "gx", "gy", "gz"),
    )
    out_specs = (P(None, "gx", "gy", "gz"), P(None, "gx", "gy", "gz"))
    return jax.shard_map(
        on_device, mesh=mesh, in_specs=in_specs, out_specs=out_specs, check_vma=False
    )
```

```python
import functools
import math

import jax
import jax.numpy as jnp
import numpy as np
from jax import lax
from jax.experimental import pallas as pl
from jax.experimental.pallas import tpu as pltpu
from jax.sharding import PartitionSpec as P

deriv_alpha = 1.0 / 3.0
filter_alpha = 0.4999
gas_gamma = 1.4
time_step = 0.2
section_a = -5.0 / 9.0
section_b = 15.0 / 16.0
explicit_weights = (0.75, -0.15, 1.0 / 60.0)
f32 = jnp.float32
CUTS = (0, 4, 12)


def root_of(coupling):
    return (-1.0 + math.sqrt(1.0 - 4.0 * coupling * coupling)) / (2.0 * coupling)


def laurent(poly, times_s):
    size = len(poly) + 1
    total = np.zeros(2 * size + 1)
    for power, value in enumerate(poly):
        term = np.array([1.0])
        for _ in range(power):
            term = np.convolve(term, [1.0, 0.0, 1.0])
        if times_s:
            term = np.convolve(term, [-1.0, 0.0, 1.0])
        half = len(term) // 2
        total[size - half : size + half + 1] += value * term
    return [float(v) for v in total[size:]]


def x_constants():
    ad, af = deriv_alpha, filter_alpha
    kappa = (1.0 / 36.0) / ad
    beta = 7.0 / 9.0 - kappa
    poly = np.polynomial.polynomial
    p_of_c = (1.0 - 2.0 * af) / 256.0 * poly.polypow([2.0, -1.0], 4)
    q_of_c, rest = poly.polydiv(p_of_c, [1.0, af])
    rho = float(rest[0])
    both = poly.polymul([1.0, af], [1.0, ad])
    q2_of_c, _ = poly.polydiv(p_of_c, both)
    mu_f = float(poly.polyval(-1.0 / af, p_of_c)) / (1.0 - ad / af)
    mu_d = float(poly.polyval(-1.0 / ad, p_of_c)) / (1.0 - af / ad)
    b_of_c = poly.polyadd(kappa * q_of_c, beta * q2_of_c)
    g = 1.0 / math.sqrt(1.0 - 4.0 * af * af)
    sigma = -section_b * time_step
    return dict(
        kappa=kappa,
        deriv=beta / ad,
        band_q=laurent(q_of_c, False)[:4],
        band_f=[sigma * v for v in laurent(b_of_c, True)[:5]],
        own=rho * g,
        pair=sigma * (kappa * rho + beta * mu_f) / af,
        slow=sigma * beta * mu_d / ad,
    )


X = x_constants()
ROOT_D = root_of(deriv_alpha)
ROOT_F = root_of(filter_alpha)


def primitives(cells):
    density, m0, m1, m2, energy = cells
    inverse = 1.0 / density
    squared = m0 * m0 + m1 * m1 + m2 * m2
    pressure = (gas_gamma - 1.0) * (energy - 0.5 * squared * inverse)
    return inverse, pressure


def flux(cells, inverse, pressure, axis_k):
    momentum = cells[1:4]
    velocity = momentum[axis_k] * inverse
    parts = [
        momentum[axis_k],
        momentum[0] * velocity,
        momentum[1] * velocity,
        momentum[2] * velocity,
        (cells[4] + pressure) * velocity,
    ]
    parts[axis_k + 1] = parts[axis_k + 1] + pressure
    return parts


def lanes(shape):
    return lax.broadcasted_iota(jnp.int32, shape, len(shape) - 1)


def roll(value, amount):
    size = value.shape[-1]
    if isinstance(amount, int):
        amount = amount % size
        if amount == 0:
            return value
    return pltpu.roll(value, amount, value.ndim - 1)


class Blocks:
    def __init__(self, sources, targets, sems, dims, size, begin=0):
        self.parts = list(zip(sources, targets, dims, strict=True))
        self.sems, self.size, self.begin = sems, size, begin
        self.count = targets[0].shape[dims[0]] // size

        def start(k, _):
            for copy in self.piece(k):
                copy.start()
            return 0

        lax.fori_loop(0, self.count, start, 0)

    def piece(self, k):
        copies = []
        for n, (source, target, dim) in enumerate(self.parts):
            lead = (slice(None),) * dim
            first = pl.multiple_of(k * self.size, self.size)
            there = source.at[(*lead, pl.ds(self.begin + first, self.size))]
            here = target.at[(*lead, pl.ds(first, self.size))]
            copies.append(pltpu.make_async_copy(there, here, self.sems.at[n, k]))
        return copies

    def wait(self, k):
        for copy in self.piece(k):
            copy.wait()

    def each(self, body, steps):
        def one(k, _):
            self.wait(k)
            lax.fori_loop(k * steps, (k + 1) * steps, body, 0)
            return 0

        lax.fori_loop(0, self.count, one, 0)


def write_out(kernel_part, pieces, copy_of):
    def one(k, _):
        kernel_part(k)
        copy_of(k).start()
        return 0

    def wait(k, _):
        copy_of(k).wait()
        return 0

    lax.fori_loop(0, pieces, one, 0)
    lax.fori_loop(0, pieces, wait, 0)


def cells_at(rho, mom, ene, x, at):
    return [rho[x, at], mom[0, x, at], mom[1, x, at], mom[2, x, at], ene[x, at]]


def face_kernel(
    rho_hbm, mom_hbm, ene_hbm,
    d_out, f_out, own, g_rows, h_rows, z_up, z_down, z_own, y_edge, token,
    rho, mom, ene, sems,
):
    nx, ny, nz = rho.shape
    lane = lanes((8, nz))
    slot = lane // 8
    first_half = lane % 8 < 4
    row = lax.broadcasted_iota(jnp.int32, (8, nz), 0)
    stored = {x: r for r, x in enumerate((0, 1, 2, nx - 3, nx - 2, nx - 1))}
    rows = 16
    blocks = Blocks((rho_hbm, mom_hbm, ene_hbm), (rho, mom, ene), sems, (1, 2, 1), rows)
    token[...] = jnp.zeros_like(token)
    odd = is_upper()

    def tile(t, _):
        at = pl.ds(pl.multiple_of(8 * t, 8), 8)
        keep = (row < 4) & (t > 0)
        packed = [[None] * 5, [None] * 5]
        totals = lower = upper = None
        for x in range(nx):
            cells = cells_at(rho, mom, ene, x, at)
            inverse, pressure = primitives(cells)
            f = flux(cells, inverse, pressure, 0)
            g = flux(cells, inverse, pressure, 1)
            h = flux(cells, inverse, pressure, 2)
            group, place = x // 16, x % 16
            for v in range(5):
                y_edge[v, x] = jnp.where(keep, y_edge[v, x], g[v])
                moved = roll(cells[v], 8 * place + 3)
                if place:
                    moved = jnp.where(slot == place, moved, packed[group][v])
                packed[group][v] = moved
                if x in stored:
                    g_rows[stored[x], v, at] = g[v]
                    h_rows[stored[x], v, at] = h[v]
                if x == 0:
                    f_out[0, v, at] = f[v]
                if x == nx - 1:
                    first = f_out[0, v, at]
                    f_out[0, v, at] = jnp.where(odd, first, f[v])
                    f_out[1, v, at] = jnp.where(odd, f[v], first)
            if x == 0:
                totals, lower, upper = [g, h, g, h], f, f
            else:
                lower = [ROOT_D * a + b for a, b in zip(lower, f)]
                upper = [a + ROOT_D**x * b for a, b in zip(upper, f)]
                factor = ROOT_F**x
                totals = [
                    [ROOT_F * a + b if k < 2 else a + factor * b for a, b in zip(total, term)]
                    for k, (total, term) in enumerate(zip(totals, (g, h, g, h)))
                ]
        h = [flux(packed[group], *primitives(packed[group]), 2) for group in range(2)]
        for v in range(5):
            d_out[0, v, at] = own[0, v, at] = lower[v]
            d_out[1, v, at] = own[1, v, at] = upper[v]
            for k in range(2):
                g_rows[6 + k, v, at] = totals[2 * k][v]
                h_rows[6 + k, v, at] = totals[2 * k + 1][v]
                y_edge[v, nx + k] = jnp.where(keep, y_edge[v, nx + k], totals[2 * k][v])
                group, place = (nx + k) // 16, (nx + k) % 16
                moved = roll(totals[2 * k + 1][v], 8 * place + 3)
                h[group][v] = jnp.where(slot == place, moved, h[group][v])
            for group in range(2):
                z_own[group, v, at] = h[group][v]
            z_up[v, at] = jnp.where(first_half, h[0][v], roll(h[1][v], 4))
            z_down[v, at] = jnp.where(first_half, roll(h[0][v], -3), roll(h[1][v], 1))
        return 0

    blocks.each(tile, rows // 8)


def base_kernel(rho_hbm, mom_hbm, ene_hbm, inc_hbm, after, base, w_up, w_down, token, rho, mom, ene, inc, sems):
    token[...] = jnp.zeros_like(token)
    nx, ny, nz = rho.shape
    rows = 16
    blocks = Blocks((rho_hbm, mom_hbm, ene_hbm, inc_hbm), (rho, mom, ene, inc), sems, (1, 2, 1, 2), rows)

    def tile(t, _):
        at = pl.ds(pl.multiple_of(8 * t, 8), 8)
        totals = None
        ends = {1.0: [[None] * 5 for _ in range(3)], -1.0: [[None] * 5 for _ in range(3)]}
        for x in range(nx):
            cells = cells_at(rho, mom, ene, x, at)
            f = flux(cells, *primitives(cells), 0)
            q = [cells[v] + (section_a * section_b) * inc[v, x, at] for v in range(5)]
            own = [X["own"] * q[v] for v in range(5)]
            pair = [X["pair"] * f[v] for v in range(5)]
            plus = [a + b for a, b in zip(own, pair)]
            minus = [a - b for a, b in zip(own, pair)]
            if x == 0:
                totals = [plus, minus]
            else:
                totals[0] = [ROOT_F * a + b for a, b in zip(totals[0], plus)]
                totals[1] = [a + ROOT_F**x * b for a, b in zip(totals[1], minus)]
            for sign, j in ((1.0, x + 1), (-1.0, nx - x)):
                for k in range(3):
                    n = k + j
                    if n > 4:
                        continue
                    for v in range(5):
                        term = (sign * X["band_f"][n]) * f[v]
                        if n <= 3:
                            term = term + X["band_q"][n] * q[v]
                        so_far = ends[sign][k][v]
                        ends[sign][k][v] = term if so_far is None else so_far + term
            if x == 3:
                for k in range(3):
                    for v in range(5):
                        w_down[k, v, at] = ends[1.0][k][v]
        for v in range(5):
            base[0, v, at] = totals[0][v]
            base[1, v, at] = totals[1][v]
            for k in range(3):
                w_up[k, v, at] = ends[-1.0][k][v]
        return 0

    blocks.each(tile, rows // 8)


def fix_table(nz):
    weight = {1: 45.0, 2: -9.0, 3: 1.0}
    table = np.zeros((4 * nz, 2 * nz))
    for group in range(2):
        for place in range(nz // 8):
            into = group * nz + 8 * place
            came = 8 * place + 4 * group
            kept = (2 + group) * nz + 8 * place
            for j in range(3):
                for n, w in weight.items():
                    if j + n >= 3:
                        table[nz + came + j + n - 3, into + j] += w
                        table[kept + 3 + j + n - 3, into + j] -= w
                    if n > j:
                        table[came + 3 + j - n, into + 3 + j] -= w
                        table[kept + 3 + j - n, into + 3 + j] += w
    return table


def split(value):
    high = value.astype(jnp.bfloat16)
    return high, (value - high.astype(f32)).astype(jnp.bfloat16)


def around(at):
    return 45.0 * (at(1) - at(-1)) - 9.0 * (at(2) - at(-2)) + (at(3) - at(-3))


def along_lanes(h):
    v1 = roll(h, -1)
    v2 = roll(v1 - 9.0 * h, -2)
    both = 9.0 * v1 - h
    return 5.0 * both + v2 + roll(both + 5.0 * v2, 3)


def turn_of(x, nz):
    if isinstance(x, int):
        return (2 * nz - 3 - 8 * (x % 16)) % nz
    return lax.rem(2 * nz - 3 - 8 * lax.rem(x, 16), nz)


def end_rows(nx):
    return [0, 1, 2, nx - 3, nx - 2, nx - 1, nx, nx + 1]


def add_cross(cross, sums, w_up, w_down):
    scale = -time_step * section_b / 60.0
    for k in range(2):
        sums[k] = sums[k] + (scale * X["own"]) * cross[6 + k]
    for w, near in ((w_down, (0, 1, 2)), (w_up, (5, 4, 3))):
        for k in range(3):
            for j in range(1, 4 - k):
                w[k] = w[k] + (scale * X["band_q"][k + j]) * cross[near[j - 1]]


def early_kernel(base, w_up0, w_down0, g_rows, h_rows, y_halo, after, sums, w_up, w_down, pad):
    ny, nz = base.shape[2:]
    nx = y_halo.shape[1] - 2
    for r, x in enumerate(end_rows(nx)):
        for v in range(5):
            pad[r, v, 0:8] = y_halo[v, x]
            pad[r, v, ny + 8 : ny + 16] = y_halo[v, x]
            pad[r, v, 8 : ny + 8] = g_rows[r, v]

    def one(v, _):
        for t in range(ny // 8):
            at = slice(8 * t, 8 * t + 8)
            cross = []
            for r in range(8):
                dy = around(lambda n, r=r, t=t: pad[r, v, 8 + 8 * t + n : 16 + 8 * t + n])
                cross.append(dy + along_lanes(h_rows[r, v, at]))
            parts = [[ref[k, v, at] for k in range(ref.shape[0])] for ref in (base, w_up0, w_down0)]
            add_cross(cross, *parts)
            for ref, part in zip((sums, w_up, w_down), parts, strict=True):
                for k, value in enumerate(part):
                    ref[k, v, at] = value
        return 0

    lax.fori_loop(0, 5, one, 0)


def end_kernel(
    nx, sums0, w_up0, w_down0, z_low, z_high, z_own, table,
    sums, own_sums, to_other, to_partner, fix, token,
):
    token[...] = jnp.zeros_like(token)
    ny, nz = sums0.shape[2:]
    lane = lanes((8, nz))
    edge_lane = (lane < 3) | (lane >= nz - 3)
    parts = [z_low[...], z_high[...], z_own[0], z_own[1]]
    halves = [split(p.reshape(5 * ny, nz)) for p in parts]
    fixed = sum(
        jnp.dot(jnp.concatenate([h[k] for h in halves], axis=1), table[...], preferred_element_type=f32)
        for k in range(2)
    )
    for group in range(2):
        fix[group] = fixed[:, group * nz : group * nz + nz].reshape(5, ny, nz)
    odd = is_upper()

    def one(v, _):
        for t in range(ny // 8):
            at = slice(8 * t, 8 * t + 8)
            cross = [
                jnp.where(edge_lane, roll(fix[x // 16, v, at], turn_of(x, nz)), 0.0) for x in end_rows(nx)
            ]
            parts = [[ref[k, v, at] for k in range(ref.shape[0])] for ref in (sums0, w_up0, w_down0)]
            add_cross(cross, *parts)
            for k in range(2):
                sums[k, v, at] = own_sums[k, v, at] = parts[0][k]
            for k in range(3):
                to_other[k, v, at] = jnp.where(odd, parts[1][k], parts[2][k])
                to_partner[k, v, at] = jnp.where(odd, parts[2][k], parts[1][k])
        return 0

    lax.fori_loop(0, 5, one, 0)


def part_kernel(
    begin, rho_hbm, mom_hbm, ene_hbm, inc_hbm, y_halo, fix, after,
    part, token,
    rho, mom, ene, inc, pad, sems,
):
    token[...] = jnp.zeros_like(token)
    nx, ny, nz = rho.shape
    lane = lanes((8, nz))
    edge_lane = (lane < 3) | (lane >= nz - 3)
    scale = -time_step / 60.0
    some = 4
    blocks = Blocks((rho_hbm, mom_hbm, ene_hbm, inc_hbm), (rho, mom, ene, inc), sems, (0, 1, 0, 1), some, begin)

    def one_row(x, _):
        turn = turn_of(begin + x, nz)
        group = (begin + x) // 16
        for v in range(5):
            pad[v, 0:8] = y_halo[v, begin + x]
            pad[v, ny + 8 : ny + 16] = y_halo[v, begin + x]
        for t in range(ny // 8):
            at = slice(8 * t, 8 * t + 8)
            cells = cells_at(rho, mom, ene, x, at)
            inverse, pressure = primitives(cells)
            g = flux(cells, inverse, pressure, 1)
            h = flux(cells, inverse, pressure, 2)
            for v in range(5):
                pad[v, 8 + 8 * t : 16 + 8 * t] = g[v]
                dz = along_lanes(h[v])
                dz = dz + jnp.where(edge_lane, roll(fix[group, v, at], turn), 0.0)
                part[v, x, at] = dz
        for t in range(ny // 8):
            at = slice(8 * t, 8 * t + 8)
            for v in range(5):
                dy = around(lambda n, v=v, t=t: pad[v, 8 + 8 * t + n : 16 + 8 * t + n])
                part[v, x, at] = section_a * inc[v, x, at] + scale * (part[v, x, at] + dy)
        return 0

    blocks.each(one_row, some)


def line_kernel(count, rho_hbm, mom_hbm, ene_hbm, f_near, *rest):
    parts, rest = rest[:count], rest[count:]
    *sums, new_inc_hbm, local, edges = rest[:-9]
    rho, mom, ene, new_inc, f_all, q_all, e_all, sems, out_sems = rest[-9:]
    nx, ny, nz = rho.shape
    rows = 16
    blocks = Blocks((rho_hbm, mom_hbm, ene_hbm), (rho, mom, ene), sems, (1, 2, 1), rows)

    def copy_of(k):
        at = pl.ds(pl.multiple_of(k * rows, rows), rows)
        return pltpu.make_async_copy(new_inc.at[:, :, at], new_inc_hbm.at[:, :, at], out_sems.at[k])

    def slab(k):
        blocks.wait(k)
        at = pl.ds(pl.multiple_of(k * rows, rows), rows)

        def fluxes_at(part, begin, x, _):
            cells = cells_at(rho, mom, ene, begin + x, at)
            for v, value in enumerate(flux(cells, *primitives(cells), 0)):
                f_all[v, begin + x] = value
                q_all[v, begin + x] = cells[v] + section_b * part[v, x, at]
            return 0

        begin = 0
        for part in parts:
            lax.fori_loop(0, part.shape[1], functools.partial(fluxes_at, part, begin), 0)
            begin += part.shape[1]
        lines_of = functools.partial(one_line, at, parts, f_near, sums, new_inc, local, edges, f_all, q_all, e_all)
        lax.fori_loop(0, 5, lines_of, 0)

    write_out(slab, ny // rows, copy_of)


def one_line(at, parts, f_near, sums, new_inc, local, edges, f_all, q_all, e_all, v, _):
    nx = f_all.shape[1]
    part_at = [(part, i) for part in parts for i in range(part.shape[1])]
    f = [f_all[v, x] for x in range(nx)]
    q = [q_all[v, x] for x in range(nx)]
    near = f_near[v, at]
    low, high = jnp.where(is_upper(), near, 0.0), jnp.where(is_upper(), 0.0, near)
    from_low, from_high = incoming(ROOT_D**nx, sums, v, at)
    forward = ROOT_D * from_low
    for x in range(nx):
        e_all[x] = forward
        forward = ROOT_D * (f[x] + forward)
    backward = ROOT_D * from_high
    for x in reversed(range(nx)):
        e_all[x] = e_all[x] - backward
        backward = ROOT_D * (f[x] + backward)
    ahead = None
    for x in range(nx):
        before = low if x == 0 else f[x - 1]
        after = high if x == nx - 1 else f[x + 1]
        e = e_all[x]
        deriv = (time_step * X["kappa"]) * (after - before) + (time_step * X["deriv"]) * e
        value = part_at[x][0][v, part_at[x][1], at] - deriv
        new_inc[v, x, at] = value
        if x in (0, nx - 1):
            edges[x // (nx - 1), v, at] = value
        total = (1.0 - X["band_q"][0] - X["own"]) * q[x] - X["slow"] * e
        total = total - section_b * deriv
        for n in range(1, 4):
            near = [q[i] for i in (x - n, x + n) if 0 <= i < nx]
            total = total - X["band_q"][n] * (near[0] if len(near) == 1 else near[0] + near[1])
        for n in range(1, 5):
            if x + n < nx and x - n >= 0:
                total = total - X["band_f"][n] * (f[x + n] - f[x - n])
            elif x + n < nx:
                total = total - X["band_f"][n] * f[x + n]
            else:
                total = total + X["band_f"][n] * f[x - n]
        if x == 3:
            total = total + X["band_f"][4] * low
        if x == nx - 4:
            total = total - X["band_f"][4] * high
        if ahead is not None:
            total = total - ahead
        local[v, x, at] = total
        plus = X["own"] * q[x] + X["pair"] * f[x]
        ahead = ROOT_F * (plus if ahead is None else plus + ahead)
    behind = None
    for x in reversed(range(nx)):
        if behind is not None:
            local[v, x, at] = local[v, x, at] - behind
        minus = X["own"] * q[x] - X["pair"] * f[x]
        behind = ROOT_F * (minus if behind is None else minus + behind)
    return 0


def is_upper():
    return lax.axis_index("gx") % 2 == 1


def incoming(rate, sums, v, at):
    if len(sums) == 1:
        return sums[0][0, v, at], sums[0][1, v, at]
    beside, pair, opposite = sums
    closure = 1.0 / (1.0 - rate**4)
    low, high = (closure * (opposite[k, v, at] + rate**2 * pair[k, v, at]) for k in range(2))
    odd = is_upper()
    return (
        jnp.where(odd, beside[0, v, at] + rate * low, low),
        jnp.where(odd, high, beside[1, v, at] + rate * high),
    )


def mix_kernel(rate, own, came, after, *rest):
    *others, out, pair, beside, token = rest
    odd = is_upper()
    token[...] = jnp.zeros_like(token)
    for v in range(5):
        upper = jnp.where(odd, own[0, v] + rate * came[0, v], came[0, v] + rate * own[0, v])
        lower = jnp.where(odd, came[1, v] + rate * own[1, v], own[1, v] + rate * came[1, v])
        out[0, v] = pair[0, v] = upper
        out[1, v] = pair[1, v] = lower
    beside[...] = came[...]
    if others:
        halos, f_came, d_came, halos_out, f_out, d_out = others
        halos_out[...] = halos[...]
        f_out[...] = f_came[...]
        d_out[...] = d_came[...]


def pass_kernel(came, after, near, onward, token):
    token[...] = jnp.zeros_like(token)
    near[...] = came[0]
    onward[...] = came[1]


def inner_kernel(local, w_partner, *rest):
    *sums, out_hbm, rim, out, sems = rest
    nx = local.shape[1]
    odd = is_upper()

    def one(v):
        low, high = incoming(ROOT_F**nx, sums, v, slice(None))
        for x in range(nx):
            value = local[v, x] - (ROOT_F ** (x + 1)) * low - (ROOT_F ** (nx - x)) * high
            if x < 3:
                value = value - jnp.where(odd, w_partner[x, v], 0.0)
            if x >= nx - 3:
                value = value - jnp.where(odd, 0.0, w_partner[nx - 1 - x, v])
            if 4 <= x < nx - 4:
                out[v, x] = value
            else:
                rim[x if x < 4 else x - nx + 8, v] = value

    inside = pl.ds(4, nx - 8)
    write_out(one, 5, lambda v: pltpu.make_async_copy(out.at[v, inside], out_hbm.at[v, inside], sems.at[v]))


def rim_kernel(before, inc_before, rim, edges, f_other, w_other, out_hbm, inc_hbm, out, inc, sems):
    nx = out_hbm.shape[1]
    odd = is_upper()
    step = time_step * X["kappa"]
    for v in range(5):
        for side in range(2):
            others = odd if side else jnp.logical_not(odd)
            sign = -1.0 if side else 1.0
            far = sign * jnp.where(others, f_other[v], 0.0)
            for k in range(4):
                value = rim[7 - k if side else k, v]
                if k < 3:
                    value = value - jnp.where(others, w_other[k, v], 0.0)
                if k == 0:
                    value = value + (section_b * step) * far
                if k == 3:
                    value = value + X["band_f"][4] * far
                out[side, v, 3 - k if side else k] = value
            inc[side, v, 0] = edges[side, v] + step * far
    copies = []
    for side in range(2):
        rows, row = pl.ds(side * (nx - 4), 4), pl.ds(side * (nx - 1), 1)
        copies.append(pltpu.make_async_copy(out.at[side], out_hbm.at[:, rows], sems.at[0, side]))
        copies.append(pltpu.make_async_copy(inc.at[side], inc_hbm.at[:, row], sems.at[1, side]))
    for copy in copies:
        copy.start()
    for copy in copies:
        copy.wait()


def shifted(value, axis, by):
    size = lax.axis_size(axis)
    return lax.ppermute(value, axis, [(i, (i + by) % size) for i in range(size)])


def ring_sums(own, rate):
    size = lax.axis_size("gx")
    gathered = lax.all_gather(own, "gx", axis=0)
    here = lax.axis_index("gx")
    member = jnp.arange(size, dtype=jnp.int32)
    table = jnp.asarray([rate**k / (1.0 - rate**size) for k in range(size)], f32)
    up = table[(here - 1 - member) % size]
    down = table[(member - here - 1) % size]
    shape = (size,) + (1,) * (own.ndim - 1)
    low = jnp.sum(up.reshape(shape) * gathered[:, 0], axis=0)
    high = jnp.sum(down.reshape(shape) * gathered[:, 1], axis=0)
    return jnp.stack([low, high])


def call(kernel, name, inputs, hbm, outputs, scratch, aliases=None):
    place = {True: pl.BlockSpec(memory_space=pltpu.HBM), False: pl.BlockSpec(memory_space=pltpu.VMEM)}
    shapes = [dims[1] if dims[0] == "hbm" else dims for dims in outputs]
    return pl.pallas_call(
        kernel,
        in_specs=[place[i < hbm] for i in range(len(inputs))],
        out_specs=[place[dims[0] == "hbm"] for dims in outputs],
        out_shape=[jax.ShapeDtypeStruct(dims, f32) for dims in shapes],
        scratch_shapes=scratch,
        input_output_aliases=aliases or {},
        compiler_params=pltpu.CompilerParams(vmem_limit_bytes=40 * 2**20),
        cost_estimate=pl.CostEstimate(flops=1000, bytes_accessed=1000, transcendentals=0),
        name=name,
    )(*[pltpu.with_memory_space_constraint(a, pltpu.HBM) if i < hbm else a for i, a in enumerate(inputs)])


def on_device(density, momentum, energy, increment):
    nx, ny, nz = density.shape
    members = lax.axis_size("gx")
    cells = nx * ny * nz
    state = (density, momentum, energy)
    face = (5, ny, nz)
    whole = (5, nx, ny, nz)

    def vmem(*dims):
        return pltpu.VMEM(dims, f32)

    def sems(*dims):
        return pltpu.SemaphoreType.DMA(dims)

    state_room = [vmem(nx, ny, nz), vmem(3, nx, ny, nz), vmem(nx, ny, nz)]

    d_out, f_out, own_d, g_rows, h_rows, z_up, z_down, z_own, y_edge, begun = call(
        face_kernel,
        "faces",
        state,
        3,
        [(2, *face), (2, *face), (2, *face), (8, *face), (8, *face), face, face, (2, *face), (5, nx + 2, 8, nz), (8, nz)],
        state_room + [sems(3, ny // 16)],
    )
    z_low = shifted(z_up, "gz", 1)
    z_high = shifted(z_down, "gz", -1)
    y_halo = shifted(y_edge, "gy", 1)

    base, w_up0, w_down0, based = call(
        base_kernel,
        "base",
        (*state, increment, begun),
        4,
        [(2, *face), (3, *face), (3, *face), (8, nz)],
        state_room + [vmem(*whole), sems(4, ny // 16)],
    )
    table = jnp.asarray(fix_table(nz), jnp.bfloat16)
    rate_d, rate_f = ROOT_D**nx, ROOT_F**nx
    token = based
    partner = [(i, i ^ 1) for i in range(members)]
    other = [(i, (i + 1 - 2 * (i % 2 == 0)) % members) for i in range(members)]
    mixed = [(2, *face), (2, *face), (8, nz)]
    if members == 4:
        d_came = lax.ppermute(d_out, "gx", partner)
        f_came = lax.ppermute(f_out, "gx", partner)
        group, d_pair, d_beside, token = call(
            functools.partial(mix_kernel, rate_d), "mixd", (own_d, d_came, based), 0, [(2, *face)] + mixed, []
        )
        d_opposite = shifted(group, "gx", 2)
    sums0, w_up1, w_down1 = call(
        early_kernel,
        "early",
        (base, w_up0, w_down0, g_rows, h_rows, y_halo, token),
        0,
        [(2, *face), (3, *face), (3, *face)],
        [vmem(8, 5, ny + 16, nz)],
    )
    sums, own_sums, w_to_other, w_to_partner, fix, ended = call(
        functools.partial(end_kernel, nx),
        "ends",
        (sums0, w_up1, w_down1, z_low, z_high, z_own, table),
        0,
        [(2, *face), (2, *face), (3, *face), (3, *face), (2, *face), (8, nz)],
        [],
    )
    token = ended
    if members == 4:
        sums_came = lax.ppermute(sums, "gx", partner)
        w_partner = lax.ppermute(w_to_partner, "gx", partner)
    else:
        odd = lax.axis_index("gx") % 2 == 1
        f_low = shifted(jnp.where(odd, f_out[1], f_out[0]), "gx", 1)
        f_high = shifted(jnp.where(odd, f_out[0], f_out[1]), "gx", -1)
        f_near, f_other = jnp.where(odd, f_low, f_high), jnp.where(odd, f_high, f_low)
        far = (ring_sums(own_d, rate_d),)
        w_low = shifted(jnp.where(odd, w_to_other, w_to_partner), "gx", 1)
        w_high = shifted(jnp.where(odd, w_to_partner, w_to_other), "gx", -1)
        w_other, w_partner = jnp.where(odd, w_high, w_low), jnp.where(odd, w_low, w_high)
    parts = []
    for begin, end in zip(CUTS, CUTS[1:] + (nx,), strict=True):
        rows = end - begin
        some_part, token = call(
            functools.partial(part_kernel, begin),
            "part%d" % begin,
            (*state, increment, y_halo, fix, token),
            4,
            [(5, rows, ny, nz), (8, nz)],
            [vmem(rows, ny, nz), vmem(3, rows, ny, nz), vmem(rows, ny, nz), vmem(5, rows, ny, nz)]
            + [vmem(5, ny + 16, nz), sems(4, rows // 4)],
        )
        parts.append(some_part)
        if len(parts) == 1 and members == 4:
            f_near, onward, token = call(pass_kernel, "pass", (f_came, token), 0, [face, face, (8, nz)], [])
            f_passed = shifted(onward, "gx", 2)
        if len(parts) == 2 and members == 4:
            w_to_other, f_other, d_opposite, group, f_pair, f_beside, token = call(
                functools.partial(mix_kernel, rate_f),
                "mixf",
                (own_sums, sums_came, token, w_to_other, f_passed, d_opposite),
                0,
                [(3, *face), face, (2, *face), (2, *face)] + mixed,
                [],
            )
            far = (d_beside, d_pair, d_opposite)
            w_other = lax.ppermute(w_to_other, "gx", other)
            from_others = (f_beside, f_pair, shifted(group, "gx", 2))
    if members != 4:
        from_others = (ring_sums(own_sums, rate_f),)
    new_inc, local, edges = call(
        functools.partial(line_kernel, len(parts)),
        "lines",
        (*state, f_near, *parts, *far),
        3,
        [("hbm", whole), whole, (2, *face)],
        state_room
        + [vmem(*whole), vmem(5, nx, 16, nz), vmem(5, nx, 16, nz), vmem(nx, 16, nz)]
        + [sems(3, ny // 16), sems(ny // 16)],
    )
    inner, rim = call(
        inner_kernel,
        "inner",
        (local, w_partner, *from_others),
        0,
        [("hbm", whole), (8, *face)],
        [vmem(*whole), sems(5)],
    )
    new_state, new_increment = call(
        rim_kernel,
        "rim",
        (inner, new_inc, rim, edges, f_other, w_other),
        2,
        [("hbm", whole), ("hbm", whole)],
        [vmem(2, 5, 4, ny, nz), vmem(2, 5, 1, ny, nz), sems(2, 2)],
        {0: 0, 1: 1},
    )
    return (new_state, new_increment)


def solution(mesh):
    in_specs = (
        P("gx", "gy", "gz"),
        P(None, "gx", "gy", "gz"),
        P("gx", "gy", "gz"),
        P(None, "gx", "gy", "gz"),
    )
    out_specs = (P(None, "gx", "gy", "gz"), P(None, "gx", "gy", "gz"))
    return jax.shard_map(
        on_device, mesh=mesh, in_specs=in_specs, out_specs=out_specs, check_vma=False
    )
```
